128 devices in a mesh: cuts: 16 (over x, z), tm: 8 (over y, core).
Axes of the slice: x: 4, y: 4, z: 4, core: 2. Of those that a mesh axis runs over, the one named last changes fastest.
Arguments:
- synthetic_traces: bfloat16 [16384, 3, 1024], P('cuts', None, 'tm'), may hold values from -6 to 6
- observed_traces: bfloat16 [16384, 3, 1024], P('cuts', None, 'tm'), may hold values from -6 to 6
- measure_window_start: int32 [16384, 3], P(('cuts', 'tm')), may hold values from 0 to 383
- measure_window_end: int32 [16384, 3], P(('cuts', 'tm')), may hold values from 640 to 1024
- tapers: float32 [5, 1024], replicated, may hold values from 0.2 to 1
- frequency_weight: float32 [512], replicated, may hold values from 0.1 to 1
- station_receiver_slice: int32 [16384, 1], P('cuts'), may hold values from 0 to 15; in each aligned block of 1024 rows (0 to 1023, 1024 to 2047, ...) at most 128 rows name the same one
- station_receiver_cell: int32 [16384], P('cuts'), may hold values from 0 to 2047
- stiffness: float32 [256, 128], P('cuts'), may hold values from 0.06 to 0.24
- attenuation: float32 [256, 128], P('cuts'), may hold values from 0.0002 to 0.03
- sample_damping_factor: float32 [1024], P('tm'), may hold values from 0.5 to 1, as said below
- forward_wave_field: bfloat16 [256, 128, 3, 1024], P('cuts', None, None, 'tm'), may hold values from -6 to 6
Outputs:
- adj_source: bfloat16 [16384, 3, 1024], P(('cuts', 'tm'))
- misfit: float32 [16384, 3], P(('cuts', 'tm'))
- kernel: float32 [256, 128], P(('cuts', 'tm'))
The draws below stay inside these ranges and needn't reach their ends.
Inputs may be any that keep to these rules, and one draw needn't show every extreme that they name: `station_receiver_slice`: in each aligned block of 1024 stations, at most 128 stations have their receiver in one slice. `station_receiver_cell`: cell index within the slice, x 128 + z with x counted from the slice's first column. `sample_damping_factor`: factor per sample.
All inputs are finite; a program needn't handle non-finite values.
Results may differ from the reference program's by a relative error of at most 0.0051.
Values may be sent and summed in bfloat16 or wider, within the bound.
No kernel may reach another device: no remote copies, remote signals or barrier semaphores. Data moves between devices by JAX's collectives and lax.ppermute only.
A program may use at most 128 MiB of HBM per device.

```python
import math
import jax
import jax.numpy as jnp
import numpy as np
from jax import lax

NT = 1024
NF = 512
TAPERS = 5
SWEEPS = 4
STA_GROUP = 1024
STATIONS = 16384
SLICES = 16
CAP = 128
CX = 16
CZ = 128
NX = 256


def draw_attenuation(key, part):
    key = jax.random.fold_in(key, 7)
    slow_key = jax.random.fold_in(key, 1)
    return jnp.exp(jax.random.uniform(slow_key, (NX, CZ), jnp.float32, math.log(0.0002), math.log(0.03)))


def draw_sample_damping_factor(key, part):
    key = jax.random.fold_in(key, 13)
    spot_key, depth_key = jax.random.split(key)
    spots = jax.random.randint(spot_key, (8,), 0, NT)
    depths = jax.random.uniform(depth_key, (8,), jnp.float32, 0.5, 0.8)
    return jnp.ones((NT,), jnp.float32).at[spots].min(depths)


def touch_ends(drawn, rng, low, high):
    dims = drawn.shape
    spot = [jax.random.randint(jax.random.fold_in(rng, axis), (), 0, dims[axis]) for axis in range(len(dims))]
    drawn = drawn.at[tuple(spot)].set(low)
    longest = dims.index(max(dims))
    spot[longest] = (spot[longest] + 1) % dims[longest]
    return drawn.at[tuple(spot)].set(high)


def block_scale(own_key, extent, cuts, smallest, top_value):
    def one(axis_at, shards_of):
        heights = jax.random.uniform(jax.random.fold_in(jax.random.fold_in(own_key, 6), axis_at), (shards_of,), jnp.float32, smallest / len(cuts), top_value / len(cuts))
        return jnp.repeat(jnp.exp(heights), extent[axis_at] // shards_of).reshape((-1,) + (1,) * (len(extent) - axis_at - 1))

    level = one(*cuts[0])
    for cut in cuts[1:]:
        level = level * one(*cut)
    return level


def deal_out(rng, own, number, rows, count, top, reach, skew):
    ranking = jax.random.permutation(rng, count)
    heavy_load, common = portions_of(count, rows * top, reach, skew, True), portions_of(count, rows * top, reach, skew, False)
    places = jnp.arange(count)

    def named(tallies, turn):
        used = int((tallies > 0).sum())
        fixed = max(1, used // 4)
        shifted = fixed + (places - fixed + turn * (used - fixed)) % max(1, count - fixed)
        return jnp.zeros((count,), jnp.int32).at[ranking[jnp.where(places < fixed, places, shifted)]].set(jnp.asarray(tallies, jnp.int32))

    tallies = jnp.where(number % 4 == 0, named(heavy_load, number // 4), named(common, number - number // 4 - 1))
    mixed = jax.random.permutation(jax.random.fold_in(own, 3), count)
    giver, taker = mixed[0:count // 2 * 2:2], mixed[1:count // 2 * 2:2]
    room = jnp.minimum(tallies[giver] - 1, reach - tallies[taker]) // 2
    room = jnp.where((giver == ranking[0]) | (taker == ranking[0]) | (tallies[taker] == 0), 0, jnp.maximum(room, 0))
    shifted = jax.random.randint(jax.random.fold_in(own, 4), (count // 2,), 0, 1 << 20) % (room + 1)
    tallies = tallies.at[giver].add(-shifted).at[taker].add(shifted)
    members = jnp.searchsorted(jnp.cumsum(tallies), jnp.arange(rows * top), side="right").astype(jnp.int32)
    table = members.reshape(top, rows).T
    table = table[jax.random.permutation(jax.random.fold_in(own, 1), rows)]
    turn = jax.random.randint(jax.random.fold_in(own, 2), (rows, 1), 0, top)
    return jnp.take_along_axis(table, (jnp.arange(top)[None, :] + turn) % top, axis=1)


def portions_of(count, total, limit, lean, full):
    loads = [(1 << 20) // math.isqrt(rank ** lean) + 1 for rank in range(1, count + 1)]
    largest = limit if full else min(limit, max(-(-total // count), total * loads[0] // sum(loads)))
    least = 1 if total - largest >= count - 1 else 0
    holding, rest = [largest] + [least] * (count - 1), total - largest - least * (count - 1)
    while rest > 0:
        movable = [i for i in range(1, count) if holding[i] < largest] or [i for i in range(1, count) if holding[i] < limit]
        mass, remaining = sum([loads[i] for i in movable]), rest
        for i in movable:
            more = min(limit - holding[i], max(1, remaining * loads[i] // mass), rest)
            holding[i] = holding[i] + more
            rest = rest - more
    return np.array(holding)


def centred(stream_key, dims, spread, reach, shards=(), kind=jnp.bfloat16):
    drawn = jax.random.normal(stream_key, dims, jnp.float32) * spread
    if len(shards) > 0:
        drawn = block_scale(stream_key, dims, shards, -0.22, 0.18) * drawn
    return jnp.clip(drawn, min=-reach, max=reach).astype(kind)


def setup_inputs(seed: int = 0) -> dict:
    streams_of = jax.random.split(jax.random.key(seed), 13)
    synthetic_traces = centred(streams_of[0], (STATIONS, 3, NT), 1.0, 6.0, ((0, 16), (2, 8)))
    observed_traces = centred(streams_of[1], (STATIONS, 3, NT), 1.0, 6.0, ((0, 16), (2, 8)))
    measure_window_start = touch_ends(jax.random.randint(streams_of[2], (STATIONS, 3), 0, 3 * NT // 8), jax.random.fold_in(streams_of[2], 1), 0, (3 * NT // 8) - 1).astype(jnp.int32)
    measure_window_end = touch_ends(jax.random.randint(streams_of[3], (STATIONS, 3), 5 * NT // 8, NT + 1), jax.random.fold_in(streams_of[3], 1), 5 * NT // 8, NT).astype(jnp.int32)
    tapers = jnp.clip(jax.random.uniform(streams_of[4], (TAPERS, NT), jnp.float32, 0.2, 1.0), 0.2, 1.0)
    frequency_weight = jnp.clip(jnp.exp(jax.random.uniform(streams_of[5], (NF,), jnp.float32, math.log(0.1), math.log(1.0))), 0.1, 1.0)
    station_receiver_slice_keys = jax.random.split(jax.random.fold_in(streams_of[6], 1), STATIONS // STA_GROUP)
    station_receiver_slice_turns = jax.random.permutation(jax.random.fold_in(streams_of[6], 3), STATIONS // STA_GROUP)
    station_receiver_slice = jax.vmap(lambda own, number: deal_out(jax.random.fold_in(streams_of[6], 2), own, number, STA_GROUP, SLICES, 1, CAP, 1))(station_receiver_slice_keys, station_receiver_slice_turns).reshape((STATIONS, 1))
    station_receiver_cell = touch_ends(jax.random.randint(streams_of[7], (STATIONS,), 0, CX * CZ), jax.random.fold_in(streams_of[7], 1), 0, (CX * CZ) - 1).astype(jnp.int32)
    stiffness = jnp.clip(jnp.exp(math.log(0.24) - 1.3862944 * jax.random.uniform(streams_of[8], (NX, CZ), jnp.float32) ** block_scale(streams_of[8], (NX, CZ), ((0, 16),), -0.2, 0.2)), 0.06, 0.24)
    attenuation = draw_attenuation(jax.random.fold_in(streams_of[12], 71), 0)
    sample_damping_factor = draw_sample_damping_factor(jax.random.fold_in(streams_of[12], 71), 0)
    forward_wave_field = centred(streams_of[11], (NX, CZ, 3, NT), 1.0, 6.0, ((0, 16), (3, 8)))
    return dict(synthetic_traces=synthetic_traces, observed_traces=observed_traces, measure_window_start=measure_window_start, measure_window_end=measure_window_end, tapers=tapers, frequency_weight=frequency_weight, station_receiver_slice=station_receiver_slice, station_receiver_cell=station_receiver_cell, stiffness=stiffness, attenuation=attenuation, sample_damping_factor=sample_damping_factor, forward_wave_field=forward_wave_field)


EPSILON = 1e-05

def dft_table(length, freq_count):
    sample_col = jnp.arange(length, dtype=jnp.int32)[:, None]
    freq_row = jnp.arange(freq_count, dtype=jnp.int32)[None, :]
    phase_angle = (sample_col * freq_row % length).astype(jnp.float32) * (2.0 * math.pi / length)
    return jnp.concatenate([jnp.cos(phase_angle), jnp.sin(phase_angle)], axis=1).astype(jnp.bfloat16)

def station_terms(synthetic, observed, starts, ends, tapers, frequency_weight, table):
    length = synthetic.shape[-1]
    sample_ids = jnp.arange(length, dtype=jnp.int32)
    window_mask = ((sample_ids >= starts[..., None]) & (sample_ids < ends[..., None])).astype(jnp.float32)
    syn_float = synthetic.astype(jnp.float32)
    windowed = window_mask * (syn_float - observed.astype(jnp.float32))
    tapered = (tapers[None, None, :, :] * windowed[:, :, None, :]).astype(jnp.bfloat16)
    tap_rows = tapered.reshape(-1, length)
    spectra = jnp.dot(tap_rows, table, preferred_element_type=jnp.float32)
    weight = jnp.concatenate([frequency_weight, frequency_weight])
    win_count = lax.optimization_barrier(jnp.sum(window_mask, axis=-1))
    energy = lax.optimization_barrier(jnp.sum(window_mask * syn_float * syn_float, axis=-1)) / win_count + EPSILON
    band_power = lax.optimization_barrier(jnp.sum((weight * spectra * spectra).reshape(synthetic.shape[0], 3, -1), axis=-1))
    misfit = band_power / (length * win_count * energy)
    weighted = (weight * spectra).astype(jnp.bfloat16)
    inverse = lax.dot_general(weighted, table, (((1,), (1,)), ((), ())), preferred_element_type=jnp.float32)
    inverse = inverse.reshape(synthetic.shape[0], 3, tapers.shape[0], length)
    summed = lax.optimization_barrier(jnp.sum(tapers[None, None, :, :] * inverse, axis=2))
    adjoint_src = (summed * window_mask * (2.0 / length) / energy[..., None]).astype(jnp.bfloat16)
    return (adjoint_src, misfit)

def compose(earlier, latter):
    return (latter[0] * earlier[0], latter[0] * earlier[1] + latter[1])

def reference(synthetic_traces, observed_traces, measure_window_start, measure_window_end, tapers, frequency_weight, station_receiver_slice, station_receiver_cell, stiffness, attenuation, sample_damping_factor, forward_wave_field):
    table = dft_table(NT, NF)

    def per_group(pieces):
        return station_terms(pieces[0], pieces[1], pieces[2], pieces[3], tapers, frequency_weight, table)
    grouped = (synthetic_traces.reshape(SLICES, STA_GROUP, 3, NT), observed_traces.reshape(SLICES, STA_GROUP, 3, NT), measure_window_start.reshape(SLICES, STA_GROUP, 3), measure_window_end.reshape(SLICES, STA_GROUP, 3))
    adj_groups, misfit_groups = lax.map(per_group, grouped)
    adj_source = adj_groups.reshape(STATIONS, 3, NT)
    misfit = misfit_groups.reshape(STATIONS, 3)
    flat_traces = adj_source.reshape(STATIONS, 3 * NT).astype(jnp.float32)
    cell_index = (station_receiver_slice[:, 0] * (CX * CZ) + station_receiver_cell).astype(jnp.int32)
    source = jax.ops.segment_sum(flat_traces, cell_index, num_segments=NX * CZ)
    wavefield = source.reshape(NX, CZ, 3, NT)
    stiff_cells = stiffness[:, :, None, None]
    for sweep_index in range(SWEEPS):
        zero_rim = jnp.zeros_like(wavefield[:, :1])
        upper_side = jnp.concatenate([wavefield[:, 1:], zero_rim], axis=1)
        lower_side = jnp.concatenate([zero_rim, wavefield[:, :-1]], axis=1)
        wavefield = wavefield + stiff_cells * (jnp.roll(wavefield, -1, 0) + jnp.roll(wavefield, 1, 0) + upper_side + lower_side - 4.0 * wavefield)
    damping_retained = jnp.exp(-attenuation)[:, :, None, None] * sample_damping_factor[None, None, None, :]
    drive = jnp.sqrt(1.0 - jnp.exp(-2.0 * attenuation))[:, :, None, None] * wavefield
    decay_total, adjoint = lax.associative_scan(compose, (damping_retained, drive), reverse=True, axis=3)
    kernel = lax.optimization_barrier(jnp.sum(forward_wave_field.astype(jnp.float32) * adjoint, axis=(2, 3))) / math.sqrt(3 * NT)
    return (adj_source, misfit, kernel)
```

```python
import math

import jax
import jax.numpy as jnp
import numpy as np
from jax import lax
from jax.experimental import pallas as pl
from jax.experimental.pallas import tpu as pltpu
from jax.sharding import PartitionSpec as P

NT = 1024
SWEEPS = 4
EPSILON = 1e-05
NTM = 8
BLK = 128
COMPS = 3
SLICES = 16
CAP = 128
HALO = 4
CX = 16
CZ = 128
EXT = CX + 2 * HALO
CT = COMPS * BLK
VMEM_BIG = 52 * 1024 * 1024

f32 = jnp.float32
bf16 = jnp.bfloat16


def call(kernel, outs, args, scratch=(), smem=0, flops=1e8, nbytes=2e6):
    specs = [
        pl.BlockSpec(memory_space=pltpu.SMEM if i < smem else pltpu.VMEM) for i in range(len(args))
    ]
    many = isinstance(outs, (list, tuple))
    return pl.pallas_call(
        kernel,
        out_shape=outs,
        in_specs=specs,
        out_specs=[pl.BlockSpec(memory_space=pltpu.VMEM)] * len(outs)
        if many
        else pl.BlockSpec(memory_space=pltpu.VMEM),
        scratch_shapes=list(scratch),
        compiler_params=pltpu.CompilerParams(vmem_limit_bytes=VMEM_BIG),
        cost_estimate=pl.CostEstimate(
            flops=int(flops), bytes_accessed=int(nbytes), transcendentals=0
        ),
    )(*args)


def shape(dims, dtype):
    return jax.ShapeDtypeStruct(dims, dtype)


def block_at(index):
    return pl.ds(pl.multiple_of(index * BLK, BLK), BLK)


def lanes(rows, cols):
    return lax.broadcasted_iota(jnp.int32, (rows, cols), 1)


def columns_of(rows):
    pad = jnp.zeros((BLK - rows.shape[0], BLK), rows.dtype)
    return jnp.transpose(jnp.concatenate([rows, pad], axis=0))


def diff_kernel(me_ref, syn_ref, obs_ref, *outs):
    me = me_ref[0]
    for k in range(NTM):
        rows = block_at(lax.rem(me + k, NTM))
        for c in range(COMPS):
            outs[k][c] = (syn_ref[c, rows, :].astype(f32) - obs_ref[c, rows, :].astype(f32)).astype(
                bf16
            )


def energy_kernel(me_ref, syn_ref, win_ref, out_ref):
    t = lanes(BLK, BLK) + me_ref[0] * BLK
    lane = lanes(BLK, BLK)
    gathered = jnp.zeros((BLK, BLK), f32)
    for m in range(NTM):
        win = columns_of(win_ref[m])
        for c in range(COMPS):
            inside = (t >= win[:, c : c + 1]) & (t < win[:, 3 + c : 4 + c])
            x = syn_ref[c, m * BLK : (m + 1) * BLK, :].astype(f32)
            col = jnp.sum(jnp.where(inside, x * x, 0.0), axis=1, keepdims=True)
            gathered = jnp.where(lane == m * 8 + c, col, gathered)
    out_ref[...] = jnp.transpose(gathered)[: NTM * 8].reshape(NTM, 8, BLK)


def operator_kernel(weight_ref, ca_ref, sa_ref, cb_ref, sb_ref, tapers_ref, out_ref):
    hi = lax.Precision.HIGHEST
    w = weight_ref[...]
    wc = jnp.dot(w, cb_ref[...], precision=hi, preferred_element_type=f32)
    ws = jnp.dot(w, sb_ref[...], precision=hi, preferred_element_type=f32)
    h = jnp.sum(ca_ref[...] * wc - sa_ref[...] * ws, axis=0, keepdims=True)
    taps = tapers_ref[...]
    for i in range(NT // BLK):
        wide = jnp.broadcast_to(h, (BLK, NT))
        ring = pltpu.roll(wide, i * BLK, 1, stride=1, stride_axis=0)
        cols = columns_of(taps[:, i * BLK : (i + 1) * BLK])
        joint = cols[:, 0:1] * taps[0:1]
        for k in range(1, 5):
            joint = joint + cols[:, k : k + 1] * taps[k : k + 1]
        out_ref[i * BLK : (i + 1) * BLK, :] = (ring * joint).astype(bf16)


def owner_kernel(me_ref, win_ref, epart_ref, oper_ref, *refs):
    blocks, adj_ref, mis_ref = refs[:NTM], refs[NTM], refs[NTM + 1]
    sends, wd_ref = refs[NTM + 2 : 2 * NTM + 1], refs[2 * NTM + 1]
    me = me_ref[0]
    win = win_ref[...]
    cols = columns_of(win)
    esum = jnp.sum(epart_ref[...], axis=0)
    count = (win[3:6] - win[0:3]).astype(f32)
    energy = esum[0:3] / count + EPSILON
    scale = columns_of((2.0 / NT) / energy)
    lane = lanes(BLK, BLK)
    for k in range(NTM):
        tau = lax.rem(me - k + NTM, NTM)
        t = lane + tau * BLK
        for c in range(COMPS):
            inside = (t >= cols[:, c : c + 1]) & (t < cols[:, 3 + c : 4 + c])
            wd_ref[c, :, block_at(tau)] = jnp.where(inside, blocks[k][c].astype(f32), 0.0).astype(
                bf16
            )
    power = jnp.zeros((BLK, BLK), f32)
    t = lanes(BLK, NT)
    for c in range(COMPS):
        wd = wd_ref[c]
        res = jnp.dot(wd, oper_ref[...], preferred_element_type=f32)
        num = jnp.sum(wd.astype(f32) * res, axis=1, keepdims=True)
        power = jnp.where(lane == c, num, power)
        inside = (t >= cols[:, c : c + 1]) & (t < cols[:, 3 + c : 4 + c])
        adj_ref[c] = jnp.where(inside, res * scale[:, c : c + 1], 0.0).astype(bf16)
    for k in range(1, NTM):
        tau = lax.rem(me + k, NTM)
        for c in range(COMPS):
            sends[k - 1][c] = adj_ref[c, :, block_at(tau)]
    mis_ref[...] = jnp.transpose(power)[0:3] / (NT * count * energy)


def slot_kernel(slice_ref, cell_ref, pick_ref, cells_ref):
    n = NT
    slices = slice_ref[...]
    hot = lax.broadcasted_iota(jnp.int32, (SLICES, n), 0) == slices
    before = lax.broadcasted_iota(jnp.int32, (n, n), 0) < lax.broadcasted_iota(jnp.int32, (n, n), 1)
    hot = hot.astype(f32)
    rank = jnp.dot(hot.astype(bf16), before.astype(f32).astype(bf16), preferred_element_type=f32)
    slot = slices * CAP + jnp.sum(hot * rank, axis=0, keepdims=True).astype(jnp.int32)
    row = lax.broadcasted_iota(jnp.int32, (CAP, n), 0)
    for s in range(SLICES):
        pick_ref[s * CAP : (s + 1) * CAP, :] = (
            (row + s * CAP == slot).astype(f32).astype(bf16)
        )
    cell = cell_ref[...]
    both = jnp.concatenate(
        [
            (cell // CZ).astype(f32),
            (cell % CZ).astype(f32),
            jnp.zeros((14, n), f32),
        ],
        axis=0,
    ).astype(bf16)
    for s in range(SLICES):
        got = lax.dot_general(
            both,
            pick_ref[s * CAP : (s + 1) * CAP, :],
            (((1,), (1,)), ((), ())),
            preferred_element_type=f32,
        )
        cells_ref[s] = got[0:8]


def pick_kernel(me_ref, pick_ref, adj_ref, *refs):
    blocks, out_ref, x_ref = refs[: NTM - 1], refs[NTM - 1], refs[NTM]
    me = me_ref[0]
    for c in range(COMPS):
        cols = slice(c * BLK, (c + 1) * BLK)
        x_ref[block_at(me), cols] = adj_ref[c, :, block_at(me)]
        for k in range(1, NTM):
            x_ref[block_at(lax.rem(me - k + NTM, NTM)), cols] = blocks[k - 1][c]
    for s in range(0, SLICES, 4):
        rows = slice(s * CAP, (s + 4) * CAP)
        out_ref[rows, :] = jnp.dot(
            pick_ref[rows, :], x_ref[...], preferred_element_type=f32
        ).astype(bf16)


def scan_kernel(left_ref, mid_ref, right_ref, att_ref, damp_ref, out_ref, head_ref):
    lane = lanes(BLK, BLK)
    damp = damp_ref[...]
    before = jnp.where(lanes(1, BLK) == 0, 0.0, pltpu.roll(damp, 1, 1))
    keep = jnp.exp(-att_ref[...])
    total = damp
    for s in (1, 2, 4, 8, 16, 32, 64):
        total = total * pltpu.roll(total, s, 1)
    heads = jnp.where(lane == COMPS * EXT, total, 0.0)
    for x in range(EXT):
        src, at = (
            (left_ref, x)
            if x < HALO
            else (mid_ref, x - HALO)
            if x < HALO + CX
            else (right_ref, x - HALO - CX)
        )
        held = keep[:, x : x + 1]
        factor = held * before
        g = [src[at, c].astype(f32) for c in range(COMPS)]
        for s in (1, 2, 4, 8, 16, 32, 64):
            g = [v + factor * pltpu.roll(v, s, 1) for v in g]
            if s < 64:
                factor = factor * pltpu.roll(factor, s, 1)
        last = held * damp[:, BLK - 1 :]
        for c in range(COMPS):
            out_ref[x, c] = g[c]
            heads = jnp.where(lane == c * EXT + x, last * g[c][:, BLK - 1 :], heads)
    head_ref[...] = heads


def enter_kernel(me_ref, own_ref, att_ref, damp_ref, local_ref, *refs):
    heads, out_ref, all_ref = refs[: NTM - 1], refs[NTM - 1], refs[NTM]
    me = me_ref[0]
    all_ref[me] = own_ref[...]
    for k in range(1, NTM):
        all_ref[lax.rem(me - k + NTM, NTM)] = heads[k - 1][...]
    att = att_ref[...]
    lane = lanes(BLK, BLK)
    whole = jnp.exp(-float(BLK) * att)
    state = jnp.zeros((BLK, BLK), f32)
    for tau in range(NTM - 1):
        head = all_ref[tau]
        total = head[:, COMPS * EXT : COMPS * EXT + 1]
        state = jnp.where(tau < me, head + whole * total * state, state)
    damp = damp_ref[...]
    first = lanes(1, BLK)
    upto = jnp.where(first == 0, 1.0, pltpu.roll(damp, 1, 1))
    for s in (1, 2, 4, 8, 16, 32, 64):
        upto = upto * jnp.where(first < s, 1.0, pltpu.roll(upto, s, 1))
    t = lane.astype(f32)
    for x in range(EXT):
        reach = jnp.exp(-att[:, x : x + 1] * t) * upto
        for c in range(COMPS):
            j = c * EXT + x
            out_ref[x, c] = local_ref[x, c] + reach * state[:, j : j + 1]


def sweep_kernel(rows_ref, cells_ref, stiff_ref, field_ref, out_ref, zhot_ref, hot_ref, a_ref, b_ref):
    slots = SLICES * CAP
    xs = cells_ref[0:1, :]
    zs = cells_ref[1:2, :]
    zrow = lax.broadcasted_iota(jnp.int32, (CZ, slots), 0)
    zhot_ref[...] = (zrow == zs.astype(jnp.int32)).astype(f32).astype(bf16)
    zero = jnp.zeros((CZ, CT), f32)
    for x in range(HALO + 1):
        a_ref[x] = zero
        b_ref[x] = zero
        a_ref[EXT + 1 - x] = zero
        b_ref[EXT + 1 - x] = zero
    group = 4
    for x in range(0, CX, group):
        for i in range(group):
            mask = (xs == float(x + i)).astype(f32).astype(bf16)
            hot_ref[i * CZ : (i + 1) * CZ, :] = zhot_ref[...] * mask
        got = jnp.dot(hot_ref[...], rows_ref[...], preferred_element_type=f32)
        for i in range(group):
            a_ref[HALO + 1 + x + i] = got[i * CZ : (i + 1) * CZ]
    zfull = lax.broadcasted_iota(jnp.int32, (CZ, BLK), 0)

    def update(src, x, c):
        cols = slice(c * BLK, (c + 1) * BLK)
        mid = src[x, :, cols]
        down = jnp.where(zfull == 0, 0.0, pltpu.roll(mid, 1, 0))
        up = jnp.where(zfull == CZ - 1, 0.0, pltpu.roll(mid, CZ - 1, 0))
        return mid + stiff_ref[x - 1] * (
            src[x + 1, :, cols] + src[x - 1, :, cols] + up + down - 4.0 * mid
        )

    src, dst = a_ref, b_ref
    for sweep in range(SWEEPS - 1):

        def step(x, carry, src=src, dst=dst):
            for c in range(COMPS):
                dst[x, :, c * BLK : (c + 1) * BLK] = update(src, x, c)
            return carry

        lax.fori_loop(HALO - sweep, HALO + CX + 1 + sweep + 1, step, 0)
        src, dst = dst, src

    def last(x, carry):
        acc = update(src, x, 0) * field_ref[x - 1, 0]
        for c in range(1, COMPS):
            acc = acc + update(src, x, c) * field_ref[x - 1, c]
        col = jnp.sum(acc, axis=1, keepdims=True)
        return jnp.where(lanes(CZ, BLK) == x - 1, col, carry)

    gathered = lax.fori_loop(1, EXT + 1, last, jnp.zeros((CZ, BLK), f32))
    out_ref[...] = jnp.transpose(gathered)[0:EXT]


def transform_tables():
    d = np.arange(NT)
    coarse = 2.0 * np.pi * ((np.arange(16)[:, None] * 32 * d) % NT) / NT
    fine = 2.0 * np.pi * ((np.arange(32)[:, None] * d) % NT) / NT
    return [
        jnp.asarray(v.astype(np.float32))
        for v in (np.cos(coarse), np.sin(coarse), np.cos(fine), np.sin(fine))
    ]


def onward(count, k):
    return [(i, (i + k) % count) for i in range(count)]


def body(
    synthetic_traces,
    observed_traces,
    measure_window_start,
    measure_window_end,
    tapers,
    frequency_weight,
    station_receiver_slice,
    station_receiver_cell,
    stiffness,
    attenuation,
    sample_damping_factor,
    forward_wave_field,
):
    me = lax.axis_index("tm").astype(jnp.int32).reshape(1)
    syn = jnp.transpose(synthetic_traces, (1, 0, 2))
    obs = jnp.transpose(observed_traces, (1, 0, 2))
    field = jnp.transpose(forward_wave_field, (0, 2, 1, 3))
    win = jnp.concatenate(
        [
            measure_window_start.T,
            measure_window_end.T,
            jnp.zeros((2, BLK), jnp.int32),
        ],
        axis=0,
    )
    piece = shape((COMPS, BLK, BLK), bf16)

    parts = call(diff_kernel, [piece] * NTM, (me, syn, obs), smem=1)
    win_all = lax.all_to_all(
        jnp.broadcast_to(win[None], (NTM, 8, BLK)), "tm", 0, 0, tiled=True
    )
    blocks = [parts[0]] + [
        lax.ppermute(parts[k], "tm", onward(NTM, k)) for k in range(1, NTM)
    ]
    shares = call(energy_kernel, shape((NTM, 8, BLK), f32), (me, syn, win_all), smem=1)
    epart = lax.all_to_all(shares, "tm", 0, 0, tiled=True)

    to_right, to_left = onward(SLICES, 1), onward(SLICES, SLICES - 1)
    left = lax.ppermute(field[CX - HALO :], "cuts", to_right)
    right = lax.ppermute(field[:HALO], "cuts", to_left)
    coef = jnp.stack([stiffness, attenuation])
    coef = jnp.concatenate(
        [
            lax.ppermute(coef[:, CX - HALO :], "cuts", to_right),
            coef,
            lax.ppermute(coef[:, :HALO], "cuts", to_left),
        ],
        axis=1,
    )
    stiff_ext = jnp.broadcast_to(coef[0][:, :, None], (EXT, CZ, BLK))
    att_ext = coef[1]
    att_cols = jnp.pad(
        jnp.concatenate([att_ext.T] * COMPS, axis=1), ((0, 0), (0, BLK - COMPS * EXT))
    )

    taps = jnp.pad(tapers, ((0, 3), (0, 0)))
    oper = call(
        operator_kernel,
        shape((NT, NT), bf16),
        (frequency_weight.reshape(16, 32), *transform_tables(), taps),
    )
    pick, cells = call(
        slot_kernel,
        [shape((SLICES * CAP, NT), bf16), shape((SLICES, 8, CAP), f32)],
        (station_receiver_slice.reshape(1, NT), station_receiver_cell.reshape(1, NT)),
    )
    cells = lax.all_to_all(cells, "cuts", 0, 0, tiled=True)
    cells = jnp.transpose(cells, (1, 0, 2)).reshape(8, SLICES * CAP)

    damp = sample_damping_factor.reshape(1, BLK)
    local, heads = call(
        scan_kernel,
        [shape((EXT, COMPS, CZ, BLK), f32), shape((CZ, BLK), f32)],
        (left, field, right, att_cols, damp),
    )
    passed = [lax.ppermute(heads, "tm", onward(NTM, k)) for k in range(1, NTM)]
    entered = call(
        enter_kernel,
        shape((EXT, COMPS, CZ, BLK), f32),
        (me, heads, att_cols, damp, local, *passed),
        scratch=[pltpu.VMEM((NTM, CZ, BLK), f32)],
        smem=1,
    )

    adj, misfit, *sends = call(
        owner_kernel,
        [shape((COMPS, BLK, NT), bf16), shape((COMPS, BLK), f32)] + [piece] * (NTM - 1),
        (me, win, epart, oper, *blocks),
        scratch=[pltpu.VMEM((COMPS, BLK, NT), bf16)],
        smem=1,
    )
    back = [lax.ppermute(sends[k - 1], "tm", onward(NTM, k)) for k in range(1, NTM)]
    rows = call(
        pick_kernel,
        shape((SLICES * CAP, CT), bf16),
        (me, pick, adj, *back),
        scratch=[pltpu.VMEM((NT, CT), bf16)],
        smem=1,
    )
    rows = lax.all_to_all(rows.reshape(SLICES, CAP, CT), "cuts", 0, 0, tiled=True)
    sums = call(
        sweep_kernel,
        shape((EXT, CZ), f32),
        (rows.reshape(SLICES * CAP, CT), cells, stiff_ext, entered),
        scratch=[
            pltpu.VMEM((CZ, SLICES * CAP), bf16),
            pltpu.VMEM((4 * CZ, SLICES * CAP), bf16),
            pltpu.VMEM((EXT + 2, CZ, CT), f32),
            pltpu.VMEM((EXT + 2, CZ, CT), f32),
        ],
    )
    sums = sums * (jnp.sqrt(1.0 - jnp.exp(-2.0 * att_ext)) / math.sqrt(COMPS * NT))

    pairs = sums.reshape(EXT // 2, 2, CZ)
    rim = jnp.concatenate(
        [pairs[10:12], jnp.zeros((4, 2, CZ), f32), pairs[0:2]], axis=0
    )
    terms = jnp.concatenate([pairs[2:10], rim], axis=1)
    terms = jnp.sum(lax.all_to_all(terms, "tm", 0, 0, tiled=True).reshape(NTM, 4, CZ), axis=0)
    routes = []
    for c in range(SLICES):
        routes += [(c * NTM + m, ((c + 1) % SLICES) * NTM + m) for m in (0, 1)]
        routes += [(c * NTM + m, ((c - 1) % SLICES) * NTM + m) for m in (6, 7)]
    kernel = terms[0:2] + lax.ppermute(terms[2:4], ("cuts", "tm"), routes)
    return (jnp.transpose(adj, (1, 0, 2)), misfit.T, kernel)


def solution(mesh):
    return jax.shard_map(
        body,
        mesh=mesh,
        in_specs=(
            P("cuts", None, "tm"),
            P("cuts", None, "tm"),
            P(("cuts", "tm"), None),
            P(("cuts", "tm"), None),
            P(),
            P(),
            P("cuts", None),
            P("cuts"),
            P("cuts", None),
            P("cuts", None),
            P("tm"),
            P("cuts", None, None, "tm"),
        ),
        out_specs=(P(("cuts", "tm"), None, None), P(("cuts", "tm"), None), P(("cuts", "tm"), None)),
        check_vma=False,
    )
```

```python
import math

import jax
import jax.numpy as jnp
import numpy as np
from jax import lax
from jax.experimental import pallas as pl
from jax.experimental.pallas import tpu as pltpu
from jax.sharding import PartitionSpec as P

NT = 1024
SWEEPS = 4
EPSILON = 1e-05
NTM = 8
BLK = 128
COMPS = 3
SLICES = 16
CAP = 128
HALO = 4
CHIPS = 4
CORES = 2
XGROUP = 4
PIECES = [(k, r) for k in range(CHIPS) for r in range(CORES)]
CX = 16
CZ = 128
EXT = CX + 2 * HALO
CT = COMPS * BLK
VMEM_BIG = 52 * 1024 * 1024
VMEM_ALL = 60 * 1024 * 1024

f32 = jnp.float32
bf16 = jnp.bfloat16


def call(kernel, outs, args, scratch=(), smem=0, hbm=(), after=(), limit=VMEM_BIG):
    count = len(args)
    vmem = pl.BlockSpec(memory_space=pltpu.VMEM)
    far = pl.BlockSpec(memory_space=pl.ANY)
    near = pl.BlockSpec(memory_space=pltpu.SMEM)
    specs = [near if i < smem else far if i in hbm else vmem for i in range(count)]

    def inner(*refs):
        kernel(*refs[:count], *refs[count + len(after) :])

    return pl.pallas_call(
        inner,
        out_shape=outs,
        in_specs=specs + [far] * len(after),
        out_specs=[vmem] * len(outs),
        scratch_shapes=list(scratch),
        compiler_params=pltpu.CompilerParams(vmem_limit_bytes=limit),
        cost_estimate=pl.CostEstimate(flops=10**7, bytes_accessed=10**5, transcendentals=0),
    )(*args, *after)


def hold(value, after):
    far = pl.BlockSpec(memory_space=pl.ANY)
    return pl.pallas_call(
        lambda *refs: None,
        out_shape=shape(value.shape, value.dtype),
        in_specs=[far, far],
        out_specs=far,
        input_output_aliases={0: 0},
    )(value, after)


def shape(dims, dtype):
    return jax.ShapeDtypeStruct(dims, dtype)


def block_at(index):
    return pl.ds(pl.multiple_of(index * BLK, BLK), BLK)


def lanes(rows, cols):
    return lax.broadcasted_iota(jnp.int32, (rows, cols), 1)


def columns_of(rows):
    pad = jnp.zeros((BLK - rows.shape[0], BLK), rows.dtype)
    return jnp.transpose(jnp.concatenate([rows, pad], axis=0))


def device_at(me, k, r):
    y, core = me // CORES, me % CORES
    return lax.rem(y + k, CHIPS) * CORES + lax.rem(core + r, CORES)


def diff_kernel(me_ref, syn_ref, obs_ref, stiff_ref, att_ref, field_ref, *refs):
    outs, (last_ref, first_ref, sems) = refs[:CHIPS], refs[CHIPS:]
    copies = []
    for i, (at, edge_ref) in enumerate(((CX - HALO, last_ref), (0, first_ref))):
        copies.append(
            pltpu.make_async_copy(
                field_ref.at[at : at + HALO], edge_ref.at[:, :, 0:CZ], sems.at[i]
            )
        )
        copies[-1].start()
        rows = []
        for ref in (stiff_ref, att_ref):
            rest = ref[at : at + HALO]
            for _ in range(3):
                part = rest.astype(bf16).astype(f32)
                rows.append(part)
                rest = rest - part
        for x in range(HALO):
            tile = [row[x : x + 1] for row in rows]
            tile.append(jnp.zeros((16 - len(rows), CZ), f32))
            tile = jnp.concatenate(tile, axis=0).astype(bf16)
            for c in range(COMPS):
                edge_ref[x, c, CZ : CZ + 16] = tile
    me = me_ref[0]
    for k in range(CHIPS):
        for r in range(CORES):
            rows = block_at(device_at(me, k, r))
            for c in range(COMPS):
                syn = syn_ref[c, rows, :]
                outs[k][r, c] = (syn.astype(f32) - obs_ref[c, rows, :].astype(f32)).astype(bf16)
                outs[k][r, COMPS + c] = syn
    for copy in copies:
        copy.wait()


def operator_kernel(weight_ref, ca_ref, sa_ref, cb_ref, sb_ref, tapers_ref, out_ref):
    hi = lax.Precision.HIGHEST
    w = weight_ref[...]
    wc = jnp.dot(w, cb_ref[...], precision=hi, preferred_element_type=f32)
    ws = jnp.dot(w, sb_ref[...], precision=hi, preferred_element_type=f32)
    h = jnp.sum(ca_ref[...] * wc - sa_ref[...] * ws, axis=0, keepdims=True)
    taps = tapers_ref[...]
    for i in range(NT // BLK):
        wide = jnp.broadcast_to(h, (BLK, NT))
        ring = pltpu.roll(wide, i * BLK, 1, stride=1, stride_axis=0)
        cols = columns_of(taps[:, i * BLK : (i + 1) * BLK])
        joint = cols[:, 0:1] * taps[0:1]
        for k in range(1, 5):
            joint = joint + cols[:, k : k + 1] * taps[k : k + 1]
        out_ref[i * BLK : (i + 1) * BLK, :] = (ring * joint).astype(bf16)


def owner_kernel(me_ref, win_ref, oper_ref, *refs):
    near, far = refs[:CHIPS], refs[CHIPS : 2 * CHIPS]
    adj_ref, mis_ref = refs[2 * CHIPS : 2 * CHIPS + 2]
    sends, wd_ref = refs[2 * CHIPS + 2 : 3 * CHIPS + 2], refs[3 * CHIPS + 2]
    me = me_ref[0]
    win = win_ref[...]
    cols = columns_of(win)
    count = (win[3:6] - win[0:3]).astype(f32)
    lane = lanes(BLK, BLK)
    gathered = jnp.zeros((BLK, BLK), f32)
    for c in range(COMPS):
        squares = jnp.zeros((BLK, BLK), f32)
        for k, r in PIECES:
            tau = device_at(me, CHIPS - k, r)
            block = (far if r else near)[k]
            t = lane + tau * BLK
            inside = (t >= cols[:, c : c + 1]) & (t < cols[:, 3 + c : 4 + c])
            wd_ref[c, :, block_at(tau)] = jnp.where(inside, block[r, c].astype(f32), 0.0).astype(
                bf16
            )
            syn = jnp.where(inside, block[r, COMPS + c].astype(f32), 0.0)
            squares = squares + syn * syn
        total = jnp.sum(squares, axis=1, keepdims=True)
        gathered = jnp.where(lane == c, total, gathered)
    energy = jnp.transpose(gathered)[0:3] / count + EPSILON
    scale = columns_of((2.0 / NT) / energy)
    power = jnp.zeros((BLK, BLK), f32)
    t = lanes(BLK, NT)
    for c in range(COMPS):
        wd = wd_ref[c]
        res = jnp.dot(wd, oper_ref[...], preferred_element_type=f32)
        num = jnp.sum(wd.astype(f32) * res, axis=1, keepdims=True)
        power = jnp.where(lane == c, num, power)
        inside = (t >= cols[:, c : c + 1]) & (t < cols[:, 3 + c : 4 + c])
        adj_ref[c] = jnp.where(inside, res * scale[:, c : c + 1], 0.0).astype(bf16)
    for k, r in PIECES:
        tau = block_at(device_at(me, k, r))
        for c in range(COMPS):
            sends[k][r, c] = adj_ref[c, :, tau]
    mis_ref[...] = jnp.transpose(power)[0:3] / (NT * count * energy)


def slot_kernel(slice_ref, cell_ref, slot_ref, codes_ref):
    n = NT
    slices = slice_ref[...]
    hot = lax.broadcasted_iota(jnp.int32, (SLICES, n), 0) == slices
    before = lax.broadcasted_iota(jnp.int32, (n, n), 0) < lax.broadcasted_iota(jnp.int32, (n, n), 1)
    hot = hot.astype(f32)
    rank = jnp.dot(hot.astype(bf16), before.astype(f32).astype(bf16), preferred_element_type=f32)
    slot = slices * CAP + jnp.sum(hot * rank, axis=0, keepdims=True).astype(jnp.int32)
    slot_ref[...] = slot
    row = lax.broadcasted_iota(jnp.int32, (CAP, n), 0)
    cell = cell_ref[...]
    both = jnp.concatenate(
        [(cell // CZ).astype(f32), (cell % CZ).astype(f32), jnp.zeros((14, n), f32)], axis=0
    ).astype(bf16)
    for s in range(SLICES):
        pick = (row + s * CAP == slot).astype(f32).astype(bf16)
        got = lax.dot_general(both, pick, (((1,), (1,)), ((), ())), preferred_element_type=f32)
        wide = jnp.concatenate([got, jnp.zeros((16, CT - CAP), f32)], axis=1)
        codes_ref[s] = wide.astype(bf16)


def pick_kernel(me_ref, slot_ref, codes_ref, head_ref, *refs):
    near, far = refs[:CHIPS], refs[CHIPS : 2 * CHIPS]
    out_ref, passed_ref, x_ref = refs[2 * CHIPS :]
    passed_ref[...] = head_ref[...]
    me = me_ref[0]
    for k, r in PIECES:
        rows = block_at(device_at(me, CHIPS - k, r))
        for c in range(COMPS):
            x_ref[rows, c * BLK : (c + 1) * BLK] = (far if r else near)[k][r, c]
    slot = slot_ref[...]
    group = 4
    row = lax.broadcasted_iota(jnp.int32, (group * CAP, NT), 0)
    for s in range(0, SLICES, group):
        pick = (row + s * CAP == slot).astype(f32).astype(bf16)
        got = jnp.dot(pick, x_ref[...], preferred_element_type=f32).astype(bf16)
        for i in range(group):
            out_ref[s + i, 0:CAP, :] = got[i * CAP : (i + 1) * CAP]
            out_ref[s + i, CAP : CAP + 16, :] = codes_ref[s + i]


def factors(damp):
    at, to = lax.broadcasted_iota(jnp.int32, (BLK, BLK), 0), lanes(BLK, BLK)
    prod = jnp.where(to > at, pltpu.roll(jnp.broadcast_to(damp, (BLK, BLK)), 1, 1), 1.0)
    for s in (1, 2, 4, 8, 16, 32, 64):
        prod = prod * jnp.where(to < s, 1.0, pltpu.roll(prod, s, 1))
    return jnp.where(to >= at, prod, 0.0)


def halves(value):
    high = value.astype(bf16)
    return high, (value - high.astype(f32)).astype(bf16)


def coefficients(left_ref, right_ref, stiff_ref, att_ref):
    sides = []
    for ref in (left_ref, right_ref):
        tiles = [ref[x, 0, CZ : CZ + 16].astype(f32) for x in range(HALO)]
        sides.append(
            [
                jnp.concatenate(
                    [(t[3 * i : 3 * i + 1] + t[3 * i + 1 : 3 * i + 2]) + t[3 * i + 2 : 3 * i + 3] for t in tiles],
                    axis=0,
                )
                for i in range(2)
            ]
        )
    return [
        jnp.concatenate([sides[0][i], ref[...], sides[1][i]], axis=0)
        for i, ref in enumerate((stiff_ref, att_ref))
    ]


def field_at(left_ref, mid_ref, right_ref, x, c):
    if x < HALO:
        return left_ref[x, c, 0:CZ].astype(f32)
    if x < HALO + CX:
        return mid_ref[x - HALO, c].astype(f32)
    return right_ref[x - HALO - CX, c, 0:CZ].astype(f32)


def head_kernel(
    left_ref, mid_ref, right_ref, stiff_ref, att_ref, damp_ref, head_ref, lhs_ref
):
    lane = lanes(BLK, BLK)
    t = lane.astype(f32)
    damp = damp_ref[...]
    steps = factors(damp)
    att = coefficients(left_ref, right_ref, stiff_ref, att_ref)[1]
    cols = columns_of(jnp.concatenate([att] * COMPS, axis=0))
    column = steps[:, BLK - 1 :] * damp[:, BLK - 1 :]
    high, low = halves(jnp.broadcast_to(column, (BLK, BLK)))
    zero = jnp.zeros((BLK, BLK), bf16)
    mat = jnp.concatenate(
        [jnp.concatenate([high, low], axis=1), jnp.concatenate([high, zero], axis=1)], axis=0
    )
    total = steps[0:1, BLK - 1 :] * damp[:, BLK - 1 :]
    heads = jnp.zeros((BLK, BLK), f32)
    for x0 in range(0, EXT, XGROUP):
        for i in range(XGROUP):
            x = x0 + i
            grow = jnp.exp(cols[:, x : x + 1] * t)
            for c in range(COMPS):
                rows = slice((i * COMPS + c) * CZ, (i * COMPS + c + 1) * CZ)
                high, low = halves(field_at(left_ref, mid_ref, right_ref, x, c) * grow)
                lhs_ref[rows, :BLK] = high
                lhs_ref[rows, BLK:] = low
        got = jnp.dot(lhs_ref[...], mat, preferred_element_type=f32)
        for i in range(XGROUP):
            for c in range(COMPS):
                part = got[(i * COMPS + c) * CZ : (i * COMPS + c + 1) * CZ]
                heads = jnp.where(
                    lane == c * EXT + x0 + i, part[:, :BLK] + part[:, BLK:], heads
                )
    heads = heads * jnp.exp(-float(BLK) * cols)
    head_ref[...] = jnp.where(lane == COMPS * EXT, total, heads)


def column_rows(x):
    return pl.ds((x % 3) * CZ * 8 + x // 3, CZ, stride=8)


def scan_kernel(
    me_ref, left_ref, mid_ref, right_ref, stiff_ref, att_ref, damp_ref, near_ref, far_ref,
    out_ref, scale_ref, lhs_ref, all_ref,
):
    me = me_ref[0]
    lane = lanes(BLK, BLK)
    t = lane.astype(f32)
    y, core = me // CORES, me % CORES
    for k in range(CHIPS):
        chip = lax.rem(y + CHIPS - k, CHIPS) * CORES
        all_ref[chip + core] = near_ref[k]
        all_ref[chip + 1 - core] = far_ref[k]
    stiff, att = coefficients(left_ref, right_ref, stiff_ref, att_ref)
    scale_ref[...] = jnp.sqrt(1.0 - jnp.exp(-2.0 * att)) * (1.0 / math.sqrt(COMPS * NT))
    cols = columns_of(jnp.concatenate([att] * COMPS + [stiff], axis=0))
    whole = jnp.exp(-float(BLK) * cols)
    state = jnp.zeros((BLK, BLK), f32)
    for tau in range(NTM - 1):
        head = all_ref[tau]
        total = head[:, COMPS * EXT : COMPS * EXT + 1]
        state = jnp.where(tau < me, head + whole * total * state, state)
    high, low = halves(factors(damp_ref[...]))
    zero = jnp.zeros((BLK, BLK), bf16)
    mat = jnp.concatenate(
        [jnp.concatenate([high, low], axis=1), jnp.concatenate([high, zero], axis=1)], axis=0
    )
    for x0 in range(0, EXT, XGROUP):
        for i in range(XGROUP):
            x = x0 + i
            grow = jnp.exp(cols[:, x : x + 1] * t)
            for c in range(COMPS):
                rows = slice((i * COMPS + c) * CZ, (i * COMPS + c + 1) * CZ)
                value = field_at(left_ref, mid_ref, right_ref, x, c) * grow
                enter = state[:, c * EXT + x : c * EXT + x + 1]
                high, low = halves(jnp.where(lane == 0, value + enter, value))
                lhs_ref[rows, :BLK] = high
                lhs_ref[rows, BLK:] = low
        got = jnp.dot(lhs_ref[...], mat, preferred_element_type=f32)
        for i in range(XGROUP):
            x = x0 + i
            shrink = jnp.exp(-cols[:, x : x + 1] * t)
            for c in range(COMPS):
                part = got[(i * COMPS + c) * CZ : (i * COMPS + c + 1) * CZ]
                out_ref[c, column_rows(x), :] = (part[:, :BLK] + part[:, BLK:]) * shrink
            at = COMPS * EXT + x
            out_ref[COMPS, column_rows(x), :] = jnp.broadcast_to(cols[:, at : at + 1], (CZ, BLK))


def sweep_kernel(me_ref, got_ref, field_far, scale_ref, *refs):
    outs, refs = refs[:CHIPS], refs[CHIPS:]
    rows_ref, src_ref, prod_ref, pair_ref, field_ref, sem = refs
    me = me_ref[0]
    copy = pltpu.make_async_copy(field_far, field_ref, sem)
    copy.start()
    codes = []
    for s in range(SLICES):
        rows_ref[s * CAP : (s + 1) * CAP, :] = got_ref[s, 0:CAP, :]
        codes.append(got_ref[s, CAP : CAP + 16, 0:CAP].astype(f32))
    codes = jnp.concatenate(codes, axis=1)
    wanted = (codes[1:2, :] * 32.0 + codes[0:1, :]).astype(jnp.int32) + HALO
    chunk = 512
    for r0 in range(0, EXT * CZ, chunk):
        at = lax.broadcasted_iota(jnp.int32, (chunk, 1), 0) + r0 % (8 * CZ)
        code = (at // 8) * 32 + 3 * (at % 8) + r0 // (8 * CZ)
        hot = (code == wanted).astype(f32).astype(bf16)
        src_ref[r0 : r0 + chunk, :] = jnp.dot(hot, rows_ref[...], preferred_element_type=f32)
    copy.wait()

    def rows_at(j, z):
        start = (j * CZ + z) * 8
        if not isinstance(start, int):
            start = pl.multiple_of(start, 8)
        return pl.ds(start, 8)

    def update(below, mid, above, z):
        new = []
        for j in range(3):
            after = mid[j + 1] if j < 2 else pltpu.roll(mid[0], 7, 0)
            ahead = mid[j - 1] if j > 0 else pltpu.roll(mid[2], 1, 0)
            around = (after + ahead) + (below[j] + above[j])
            new.append(mid[j] + field_ref[COMPS, rows_at(j, z), :] * (around - 4.0 * mid[j]))
        return tuple(new)

    zero = tuple(jnp.zeros((8, BLK), f32) for _ in range(3))
    for c in range(COMPS):
        cols = slice(c * BLK, (c + 1) * BLK)

        def step(u, held, first=False, past=False, c=c, cols=cols):
            if past and u >= CZ:
                row = zero
            else:
                row = tuple(src_ref[rows_at(j, u), cols] for j in range(3))
            now = []
            for level in range(SWEEPS):
                older, newer = held[level]
                now.append((newer, row))
                z = u - level - 1
                if (first and z < 0) or (past and z >= CZ):
                    row = zero
                    if first:
                        now += list(held[level + 1 :])
                        return tuple(now)
                    continue
                row = update(older, newer, row, z)
            z = u - SWEEPS
            for j in range(3):
                term = row[j] * field_ref[c, rows_at(j, z), :]
                if c > 0:
                    term = term + prod_ref[rows_at(j, z), :]
                prod_ref[rows_at(j, z), :] = term
            return tuple(now)

        held = tuple((zero, zero) for _ in range(SWEEPS))
        for u in range(SWEEPS):
            held = step(u, held, first=True)

        def steps(i, held, step=step):
            for q in range(4):
                held = step(SWEEPS + i * 4 + q, held)
            return held

        held = lax.fori_loop(0, (CZ - SWEEPS) // 4, steps, held)
        for u in range(CZ, CZ + SWEEPS):
            held = step(u, held, past=True)
    gathered = jnp.zeros((CZ, BLK), f32)
    for x in range(EXT):
        col = jnp.sum(prod_ref[column_rows(x), :], axis=1, keepdims=True)
        gathered = jnp.where(lanes(CZ, BLK) == x, col, gathered)
    sums = jnp.transpose(gathered)[0:EXT] * scale_ref[...]
    for p in range(EXT // 2):
        pair_ref[p, 0:2, :] = sums[2 * p : 2 * p + 2]
    none = jnp.zeros((4, CZ), f32)
    y, core = me // CORES, me % CORES
    for k in range(CHIPS):
        for r in range(CORES):
            m = lax.rem(y + k, CHIPS) * CORES + lax.rem(core + r, CORES)
            own = pair_ref[HALO // 2 + m, 0:2, :]
            edge = jnp.where(m < 2, (HALO + CX) // 2 + m, jnp.maximum(m - 6, 0))
            rim = jnp.where((m < 2) | (m >= 6), pair_ref[edge, 0:2, :], 0.0)
            outs[k][r] = jnp.concatenate([own, rim, none], axis=0)


def transform_tables():
    d = np.arange(NT)
    coarse = 2.0 * np.pi * ((np.arange(16)[:, None] * 32 * d) % NT) / NT
    fine = 2.0 * np.pi * ((np.arange(32)[:, None] * d) % NT) / NT
    return [
        jnp.asarray(v.astype(np.float32))
        for v in (np.cos(coarse), np.sin(coarse), np.cos(fine), np.sin(fine))
    ]


def onward(count, k):
    return [(i, (i + k) % count) for i in range(count)]


def body(
    synthetic_traces,
    observed_traces,
    measure_window_start,
    measure_window_end,
    tapers,
    frequency_weight,
    station_receiver_slice,
    station_receiver_cell,
    stiffness,
    attenuation,
    sample_damping_factor,
    forward_wave_field,
):
    me = lax.axis_index("tm").astype(jnp.int32).reshape(1)
    syn = jnp.transpose(synthetic_traces, (1, 0, 2))
    obs = jnp.transpose(observed_traces, (1, 0, 2))
    field = jnp.transpose(forward_wave_field, (0, 2, 1, 3))
    win = jnp.concatenate(
        [measure_window_start.T, measure_window_end.T, jnp.zeros((2, BLK), jnp.int32)], axis=0
    )
    routes = [
        [(i, ((i // CORES + k) % CHIPS) * CORES + i % CORES) for i in range(NTM)]
        for k in range(CHIPS)
    ]

    def swap(value):
        return lax.ppermute(value, "tm", [(i, i ^ 1) for i in range(NTM)])

    def along(values):
        return [values[0]] + [lax.ppermute(values[k], "tm", routes[k]) for k in range(1, CHIPS)]

    to_right, to_left = onward(SLICES, 1), onward(SLICES, SLICES - 1)
    sent = shape((CORES, 2 * COMPS, BLK, BLK), bf16)
    edge = shape((HALO, COMPS, CZ + 16, BLK), bf16)
    *parts, last, first = call(
        diff_kernel,
        [sent] * CHIPS + [edge, edge],
        (me, syn, obs, stiffness, attenuation, field),
        scratch=[pltpu.SemaphoreType.DMA((2,))],
        smem=1,
        hbm=(5,),
    )
    near = along(parts)
    slot, codes = call(
        slot_kernel,
        [shape((1, NT), jnp.int32), shape((SLICES, 16, CT), bf16)],
        (station_receiver_slice.reshape(1, NT), station_receiver_cell.reshape(1, NT)),
        after=(parts[0],),
    )
    left = lax.ppermute(last, "cuts", to_right)
    right = lax.ppermute(first, "cuts", to_left)
    taps = jnp.pad(tapers, ((0, 3), (0, 0)))
    (oper,) = call(
        operator_kernel,
        [shape((NT, NT), bf16)],
        (frequency_weight.reshape(16, 32), *transform_tables(), taps),
        after=(codes,),
    )
    damp = sample_damping_factor.reshape(1, BLK)
    (heads,) = call(
        head_kernel,
        [shape((CZ, BLK), f32)],
        (left, field, right, stiffness, attenuation, damp),
        scratch=[pltpu.VMEM((XGROUP * COMPS * CZ, 2 * BLK), bf16)],
        after=(oper,),
    )

    near = [near[0]] + [hold(v, heads) for v in near[1:]]
    far = [swap(v) for v in near]

    adj, misfit, *sends = call(
        owner_kernel,
        [shape((COMPS, BLK, NT), bf16), shape((COMPS, BLK), f32)]
        + [shape((CORES, COMPS, BLK, BLK), bf16)] * CHIPS,
        (me, win, oper, *near, *far),
        scratch=[pltpu.VMEM((COMPS, BLK, NT), bf16)],
        smem=1,
        after=(heads,),
        limit=VMEM_ALL,
    )
    near = along(sends)
    rows, heads = call(
        pick_kernel,
        [shape((SLICES, CAP + 16, CT), bf16), shape((CZ, BLK), f32)],
        (me, slot, codes, heads, *near, *[swap(v) for v in near]),
        scratch=[pltpu.VMEM((NT, CT), bf16)],
        smem=1,
    )
    rows = lax.all_to_all(rows, "cuts", 0, 0, tiled=True)
    heads = jnp.stack(along([heads] * CHIPS))
    entered, scale = call(
        scan_kernel,
        [shape((COMPS + 1, EXT * CZ, BLK), f32), shape((EXT, CZ), f32)],
        (me, left, field, right, stiffness, attenuation, damp, heads, swap(heads)),
        scratch=[
            pltpu.VMEM((XGROUP * COMPS * CZ, 2 * BLK), bf16),
            pltpu.VMEM((NTM, CZ, BLK), f32),
        ],
        smem=1,
    )
    terms = call(
        sweep_kernel,
        [shape((CORES, 8, CZ), f32)] * CHIPS,
        (me, rows, entered, scale),
        scratch=[
            pltpu.VMEM((SLICES * CAP, CT), bf16),
            pltpu.VMEM((EXT * CZ, CT), f32),
            pltpu.VMEM((EXT * CZ, BLK), f32),
            pltpu.VMEM((EXT // 2, 8, CZ), f32),
            pltpu.VMEM((COMPS + 1, EXT * CZ, BLK), f32),
            pltpu.SemaphoreType.DMA,
        ],
        smem=1,
        hbm=(2,),
    )

    terms = along(terms)
    terms = terms[0] + terms[1] + terms[2] + terms[3]
    straight, crossed = [], []
    for c in range(SLICES):
        for q in range(CORES):
            for m, to in ((q, (c + 1) % SLICES), (NTM - CORES + q, (c - 1) % SLICES)):
                straight.append((c * NTM + m, to * NTM + m))
                crossed.append((c * NTM + m, to * NTM + (m ^ 1)))
    kernel = (
        terms[0, 0:2]
        + swap(terms)[1, 0:2]
        + lax.ppermute(terms, ("cuts", "tm"), straight)[0, 2:4]
        + lax.ppermute(terms, ("cuts", "tm"), crossed)[1, 2:4]
    )
    return (jnp.transpose(adj, (1, 0, 2)), misfit.T, kernel)


def solution(mesh):
    return jax.shard_map(
        body,
        mesh=mesh,
        in_specs=(
            P("cuts", None, "tm"),
            P("cuts", None, "tm"),
            P(("cuts", "tm"), None),
            P(("cuts", "tm"), None),
            P(),
            P(),
            P("cuts", None),
            P("cuts"),
            P("cuts", None),
            P("cuts", None),
            P("tm"),
            P("cuts", None, None, "tm"),
        ),
        out_specs=(P(("cuts", "tm"), None, None), P(("cuts", "tm"), None), P(("cuts", "tm"), None)),
        check_vma=False,
    )
```

```python
import math

import jax
import jax.numpy as jnp
import numpy as np
from jax import lax
from jax.experimental import pallas as pl
from jax.experimental.pallas import tpu as pltpu
from jax.sharding import PartitionSpec as P

NT = 1024
SWEEPS = 4
EPSILON = 1e-05
NTM = 8
BLK = 128
COMPS = 3
SLICES = 16
CAP = 128
HALO = 4
CHIPS = 4
CORES = 2
XGROUP = 4
UNROLL = 31
PIECES = [(k, r) for k in range(CHIPS) for r in range(CORES)]
CX = 16
CZ = 128
EXT = CX + 2 * HALO
CT = COMPS * BLK
VMEM_BIG = 52 * 1024 * 1024
VMEM_ALL = 63 * 1024 * 1024

f32 = jnp.float32
bf16 = jnp.bfloat16


def call(kernel, outs, args, scratch=(), smem=0, hbm=(), after=(), limit=VMEM_BIG):
    count = len(args)
    vmem = pl.BlockSpec(memory_space=pltpu.VMEM)
    far = pl.BlockSpec(memory_space=pl.ANY)
    near = pl.BlockSpec(memory_space=pltpu.SMEM)
    specs = [near if i < smem else far if i in hbm else vmem for i in range(count)]

    def inner(*refs):
        kernel(*refs[:count], *refs[count + len(after) :])

    return pl.pallas_call(
        inner,
        out_shape=outs,
        in_specs=specs + [far] * len(after),
        out_specs=[vmem] * len(outs),
        scratch_shapes=list(scratch),
        compiler_params=pltpu.CompilerParams(vmem_limit_bytes=limit),
        cost_estimate=pl.CostEstimate(flops=10**7, bytes_accessed=10**5, transcendentals=0),
    )(*args, *after)


def hold(value, after):
    far = pl.BlockSpec(memory_space=pl.ANY)
    return pl.pallas_call(
        lambda *refs: None,
        out_shape=shape(value.shape, value.dtype),
        in_specs=[far, far],
        out_specs=far,
        input_output_aliases={0: 0},
    )(value, after)


def shape(dims, dtype):
    return jax.ShapeDtypeStruct(dims, dtype)


def block_at(index):
    return pl.ds(pl.multiple_of(index * BLK, BLK), BLK)


def lanes(rows, cols):
    return lax.broadcasted_iota(jnp.int32, (rows, cols), 1)


def columns_of(rows):
    pad = jnp.zeros((BLK - rows.shape[0], BLK), rows.dtype)
    return jnp.transpose(jnp.concatenate([rows, pad], axis=0))


def device_at(me, k, r):
    y, core = me // CORES, me % CORES
    return lax.rem(y + k, CHIPS) * CORES + lax.rem(core + r, CORES)


def diff_kernel(me_ref, syn_ref, obs_ref, *outs):
    me = me_ref[0]
    for k in range(CHIPS):
        for r in range(CORES):
            rows = block_at(device_at(me, k, r))
            for c in range(COMPS):
                syn = syn_ref[c, rows, :]
                outs[k][r, c] = (syn.astype(f32) - obs_ref[c, rows, :].astype(f32)).astype(bf16)
                outs[k][r, COMPS + c] = syn


def edge_kernel(stiff_ref, att_ref, field_ref, last_ref, first_ref, sems):
    copies = []
    for i, (at, edge_ref) in enumerate(((CX - HALO, last_ref), (0, first_ref))):
        copies.append(
            pltpu.make_async_copy(
                field_ref.at[at : at + HALO], edge_ref.at[:, :, 0:CZ], sems.at[i]
            )
        )
        copies[-1].start()
        rows = []
        for ref in (stiff_ref, att_ref):
            rest = ref[at : at + HALO]
            for _ in range(3):
                part = rest.astype(bf16).astype(f32)
                rows.append(part)
                rest = rest - part
        for x in range(HALO):
            tile = [row[x : x + 1] for row in rows]
            tile.append(jnp.zeros((16 - len(rows), CZ), f32))
            tile = jnp.concatenate(tile, axis=0).astype(bf16)
            for c in range(COMPS):
                edge_ref[x, c, CZ : CZ + 16] = tile
    for copy in copies:
        copy.wait()


def operator_kernel(weight_ref, ca_ref, sa_ref, cb_ref, sb_ref, tapers_ref, out_ref):
    hi = lax.Precision.HIGHEST
    w = weight_ref[...]
    wc = jnp.dot(w, cb_ref[...], precision=hi, preferred_element_type=f32)
    ws = jnp.dot(w, sb_ref[...], precision=hi, preferred_element_type=f32)
    h = jnp.sum(ca_ref[...] * wc - sa_ref[...] * ws, axis=0, keepdims=True)
    taps = tapers_ref[...]
    for i in range(NT // BLK):
        wide = jnp.broadcast_to(h, (BLK, NT))
        ring = pltpu.roll(wide, i * BLK, 1, stride=1, stride_axis=0)
        cols = columns_of(taps[:, i * BLK : (i + 1) * BLK])
        joint = cols[:, 0:1] * taps[0:1]
        for k in range(1, 5):
            joint = joint + cols[:, k : k + 1] * taps[k : k + 1]
        out_ref[i * BLK : (i + 1) * BLK, :] = (ring * joint).astype(bf16)


def owner_kernel(me_ref, win_ref, oper_ref, *refs):
    near, far = refs[:CHIPS], refs[CHIPS : 2 * CHIPS]
    adj_ref, mis_ref = refs[2 * CHIPS : 2 * CHIPS + 2]
    sends, (wd_ref, res_ref) = refs[2 * CHIPS + 2 : 3 * CHIPS + 2], refs[3 * CHIPS + 2 :]
    me = me_ref[0]
    win = win_ref[...]
    cols = columns_of(win)
    count = (win[3:6] - win[0:3]).astype(f32)
    lane = lanes(BLK, BLK)
    gathered = jnp.zeros((BLK, BLK), f32)
    for c in range(COMPS):
        squares = jnp.zeros((BLK, BLK), f32)
        for k, r in PIECES:
            tau = device_at(me, CHIPS - k, r)
            block = (far if r else near)[k]
            t = lane + tau * BLK
            inside = (t >= cols[:, c : c + 1]) & (t < cols[:, 3 + c : 4 + c])
            wd_ref[c * BLK : (c + 1) * BLK, block_at(tau)] = jnp.where(
                inside, block[r, c].astype(f32), 0.0
            ).astype(bf16)
            syn = jnp.where(inside, block[r, COMPS + c].astype(f32), 0.0)
            squares = squares + syn * syn
        total = jnp.sum(squares, axis=1, keepdims=True)
        gathered = jnp.where(lane == c, total, gathered)
    energy = jnp.transpose(gathered)[0:3] / count + EPSILON
    scale = columns_of((2.0 / NT) / energy)
    power = jnp.zeros((BLK, BLK), f32)
    t = lanes(BLK, NT)
    res_ref[...] = jnp.dot(wd_ref[...], oper_ref[...], preferred_element_type=f32)
    for c in range(COMPS):
        wd = wd_ref[c * BLK : (c + 1) * BLK]
        res = res_ref[c * BLK : (c + 1) * BLK]
        num = jnp.sum(wd.astype(f32) * res, axis=1, keepdims=True)
        power = jnp.where(lane == c, num, power)
        inside = (t >= cols[:, c : c + 1]) & (t < cols[:, 3 + c : 4 + c])
        adj_ref[c] = jnp.where(inside, res * scale[:, c : c + 1], 0.0).astype(bf16)
    for k, r in PIECES:
        tau = block_at(device_at(me, k, r))
        for c in range(COMPS):
            sends[k][r, c] = adj_ref[c, :, tau]
    mis_ref[...] = jnp.transpose(power)[0:3] / (NT * count * energy)


def slot_kernel(slice_ref, cell_ref, slot_ref, codes_ref):
    n = NT
    slices = slice_ref[...]
    hot = lax.broadcasted_iota(jnp.int32, (SLICES, n), 0) == slices
    before = lax.broadcasted_iota(jnp.int32, (n, n), 0) < lax.broadcasted_iota(jnp.int32, (n, n), 1)
    hot = hot.astype(f32)
    rank = jnp.dot(hot.astype(bf16), before.astype(f32).astype(bf16), preferred_element_type=f32)
    slot = slices * CAP + jnp.sum(hot * rank, axis=0, keepdims=True).astype(jnp.int32)
    slot_ref[...] = slot
    row = lax.broadcasted_iota(jnp.int32, (CAP, n), 0)
    cell = cell_ref[...]
    both = jnp.concatenate(
        [(cell // CZ).astype(f32), (cell % CZ).astype(f32), jnp.zeros((14, n), f32)], axis=0
    ).astype(bf16)
    for s in range(SLICES):
        pick = (row + s * CAP == slot).astype(f32).astype(bf16)
        got = lax.dot_general(both, pick, (((1,), (1,)), ((), ())), preferred_element_type=f32)
        wide = jnp.concatenate([got, jnp.zeros((16, CT - CAP), f32)], axis=1)
        codes_ref[s] = wide.astype(bf16)


def pick_kernel(me_ref, slot_ref, codes_ref, *refs):
    near, far = refs[:CHIPS], refs[CHIPS : 2 * CHIPS]
    out_ref, token_ref, x_ref = refs[2 * CHIPS :]
    token_ref[...] = jnp.zeros((8, BLK), f32)
    me = me_ref[0]
    for k, r in PIECES:
        rows = block_at(device_at(me, CHIPS - k, r))
        for c in range(COMPS):
            x_ref[rows, c * BLK : (c + 1) * BLK] = (far if r else near)[k][r, c]
    slot = slot_ref[...]
    group = 4
    row = lax.broadcasted_iota(jnp.int32, (group * CAP, NT), 0)
    for s in range(0, SLICES, group):
        pick = (row + s * CAP == slot).astype(f32).astype(bf16)
        got = jnp.dot(pick, x_ref[...], preferred_element_type=f32).astype(bf16)
        for i in range(group):
            out_ref[s + i, 0:CAP, :] = got[i * CAP : (i + 1) * CAP]
            out_ref[s + i, CAP : CAP + 16, :] = codes_ref[s + i]


def factors(damp):
    at, to = lax.broadcasted_iota(jnp.int32, (BLK, BLK), 0), lanes(BLK, BLK)
    prod = jnp.where(to > at, pltpu.roll(jnp.broadcast_to(damp, (BLK, BLK)), 1, 1), 1.0)
    for s in (1, 2, 4, 8, 16, 32, 64):
        prod = prod * jnp.where(to < s, 1.0, pltpu.roll(prod, s, 1))
    return jnp.where(to >= at, prod, 0.0)


def halves(value):
    high = value.astype(bf16)
    return high, (value - high.astype(f32)).astype(bf16)


def coefficients(left_ref, right_ref, stiff_ref, att_ref):
    sides = []
    for ref in (left_ref, right_ref):
        tiles = [ref[x, 0, CZ : CZ + 16].astype(f32) for x in range(HALO)]
        sides.append(
            [
                jnp.concatenate(
                    [(t[3 * i : 3 * i + 1] + t[3 * i + 1 : 3 * i + 2]) + t[3 * i + 2 : 3 * i + 3] for t in tiles],
                    axis=0,
                )
                for i in range(2)
            ]
        )
    return [
        jnp.concatenate([sides[0][i], ref[...], sides[1][i]], axis=0)
        for i, ref in enumerate((stiff_ref, att_ref))
    ]


def field_at(left_ref, mid_ref, right_ref, x, c):
    if x < HALO:
        return left_ref[x, c, 0:CZ].astype(f32)
    if x < HALO + CX:
        return mid_ref[x - HALO, c].astype(f32)
    return right_ref[x - HALO - CX, c, 0:CZ].astype(f32)


def head_kernel(
    left_ref, mid_ref, right_ref, stiff_ref, att_ref, damp_ref, head_ref, lhs_ref
):
    lane = lanes(BLK, BLK)
    t = lane.astype(f32)
    damp = damp_ref[...]
    steps = factors(damp)
    att = coefficients(left_ref, right_ref, stiff_ref, att_ref)[1]
    cols = columns_of(jnp.concatenate([att] * COMPS, axis=0))
    column = steps[:, BLK - 1 :] * damp[:, BLK - 1 :]
    high, low = halves(jnp.broadcast_to(column, (BLK, BLK)))
    zero = jnp.zeros((BLK, BLK), bf16)
    mat = jnp.concatenate(
        [jnp.concatenate([high, low], axis=1), jnp.concatenate([high, zero], axis=1)], axis=0
    )
    total = steps[0:1, BLK - 1 :] * damp[:, BLK - 1 :]
    heads = jnp.zeros((BLK, BLK), f32)
    for x0 in range(0, EXT, XGROUP):
        for i in range(XGROUP):
            x = x0 + i
            grow = jnp.exp(cols[:, x : x + 1] * t)
            for c in range(COMPS):
                rows = slice((i * COMPS + c) * CZ, (i * COMPS + c + 1) * CZ)
                high, low = halves(field_at(left_ref, mid_ref, right_ref, x, c) * grow)
                lhs_ref[rows, :BLK] = high
                lhs_ref[rows, BLK:] = low
        got = jnp.dot(lhs_ref[...], mat, preferred_element_type=f32)
        for i in range(XGROUP):
            for c in range(COMPS):
                part = got[(i * COMPS + c) * CZ : (i * COMPS + c + 1) * CZ]
                heads = jnp.where(
                    lane == c * EXT + x0 + i, part[:, :BLK] + part[:, BLK:], heads
                )
    heads = heads * jnp.exp(-float(BLK) * cols)
    head_ref[...] = jnp.where(lane == COMPS * EXT, total, heads)


def column_rows(x):
    return pl.ds((x % 3) * CZ * 8 + x // 3, CZ, stride=8)


def scan_kernel(
    me_ref, left_ref, mid_ref, right_ref, stiff_ref, att_ref, damp_ref, near_ref, far_ref,
    out_ref, scale_ref, lhs_ref, all_ref,
):
    me = me_ref[0]
    lane = lanes(BLK, BLK)
    t = lane.astype(f32)
    y, core = me // CORES, me % CORES
    for k in range(CHIPS):
        chip = lax.rem(y + CHIPS - k, CHIPS) * CORES
        all_ref[chip + core] = near_ref[k]
        all_ref[chip + 1 - core] = far_ref[k]
    stiff, att = coefficients(left_ref, right_ref, stiff_ref, att_ref)
    scale_ref[...] = jnp.sqrt(1.0 - jnp.exp(-2.0 * att)) * (1.0 / math.sqrt(COMPS * NT))
    cols = columns_of(jnp.concatenate([att] * COMPS + [stiff], axis=0))
    whole = jnp.exp(-float(BLK) * cols)
    state = jnp.zeros((BLK, BLK), f32)
    for tau in range(NTM - 1):
        head = all_ref[tau]
        total = head[:, COMPS * EXT : COMPS * EXT + 1]
        state = jnp.where(tau < me, head + whole * total * state, state)
    high, low = halves(factors(damp_ref[...]))
    zero = jnp.zeros((BLK, BLK), bf16)
    mat = jnp.concatenate(
        [jnp.concatenate([high, low], axis=1), jnp.concatenate([high, zero], axis=1)], axis=0
    )
    for x0 in range(0, EXT, XGROUP):
        for i in range(XGROUP):
            x = x0 + i
            grow = jnp.exp(cols[:, x : x + 1] * t)
            for c in range(COMPS):
                rows = slice((i * COMPS + c) * CZ, (i * COMPS + c + 1) * CZ)
                value = field_at(left_ref, mid_ref, right_ref, x, c) * grow
                enter = state[:, c * EXT + x : c * EXT + x + 1]
                high, low = halves(jnp.where(lane == 0, value + enter, value))
                lhs_ref[rows, :BLK] = high
                lhs_ref[rows, BLK:] = low
        got = jnp.dot(lhs_ref[...], mat, preferred_element_type=f32)
        for i in range(XGROUP):
            x = x0 + i
            shrink = jnp.exp(-cols[:, x : x + 1] * t)
            for c in range(COMPS):
                part = got[(i * COMPS + c) * CZ : (i * COMPS + c + 1) * CZ]
                out_ref[c, column_rows(x), :] = (part[:, :BLK] + part[:, BLK:]) * shrink
            at = COMPS * EXT + x
            out_ref[COMPS, column_rows(x), :] = jnp.broadcast_to(cols[:, at : at + 1], (CZ, BLK))


def sweep_kernel(me_ref, got_ref, field_far, scale_ref, *refs):
    out_ref, rows_ref, src_ref, prod_ref, field_ref, sem = refs
    copy = pltpu.make_async_copy(field_far, field_ref, sem)
    copy.start()
    codes = []
    for s in range(SLICES):
        rows_ref[s * CAP : (s + 1) * CAP, :] = got_ref[s, 0:CAP, :]
        codes.append(got_ref[s, CAP : CAP + 16, 0:CAP].astype(f32))
    codes = jnp.concatenate(codes, axis=1)
    wanted = (codes[1:2, :] * 32.0 + codes[0:1, :]).astype(jnp.int32) + HALO
    chunk = 512
    for r0 in range(0, EXT * CZ, chunk):
        at = lax.broadcasted_iota(jnp.int32, (chunk, 1), 0) + r0 % (8 * CZ)
        code = (at // 8) * 32 + 3 * (at % 8) + r0 // (8 * CZ)
        hot = (code == wanted).astype(f32).astype(bf16)
        src_ref[r0 : r0 + chunk, :] = jnp.dot(hot, rows_ref[...], preferred_element_type=f32)
    copy.wait()

    def rows_at(j, z):
        start = (j * CZ + z) * 8
        if not isinstance(start, int):
            start = pl.multiple_of(start, 8)
        return pl.ds(start, 8)

    def update(below, mid, above, z):
        new = []
        for j in range(3):
            after = mid[j + 1] if j < 2 else pltpu.roll(mid[0], 7, 0)
            ahead = mid[j - 1] if j > 0 else pltpu.roll(mid[2], 1, 0)
            around = (after + ahead) + (below[j] + above[j])
            new.append(mid[j] + field_ref[COMPS, rows_at(j, z), :] * (around - 4.0 * mid[j]))
        return tuple(new)

    zero = tuple(jnp.zeros((8, BLK), f32) for _ in range(3))
    for c in range(COMPS):
        cols = slice(c * BLK, (c + 1) * BLK)

        def step(u, held, first=False, past=False, c=c, cols=cols):
            if past and u >= CZ:
                row = zero
            else:
                row = tuple(src_ref[rows_at(j, u), cols] for j in range(3))
            now = []
            for level in range(SWEEPS):
                older, newer = held[level]
                now.append((newer, row))
                z = u - level - 1
                if (first and z < 0) or (past and z >= CZ):
                    row = zero
                    if first:
                        now += list(held[level + 1 :])
                        return tuple(now)
                    continue
                row = update(older, newer, row, z)
            z = u - SWEEPS
            for j in range(3):
                term = row[j] * field_ref[c, rows_at(j, z), :]
                if c > 0:
                    term = term + prod_ref[rows_at(j, z), :]
                prod_ref[rows_at(j, z), :] = term
            return tuple(now)

        held = tuple((zero, zero) for _ in range(SWEEPS))
        for u in range(SWEEPS):
            held = step(u, held, first=True)

        def steps(i, held, step=step):
            for q in range(UNROLL):
                held = step(SWEEPS + i * UNROLL + q, held)
            return held

        held = lax.fori_loop(0, (CZ - SWEEPS) // UNROLL, steps, held)
        for u in range(CZ, CZ + SWEEPS):
            held = step(u, held, past=True)
    gathered = jnp.zeros((CZ, BLK), f32)
    for x in range(EXT):
        col = jnp.sum(prod_ref[column_rows(x), :], axis=1, keepdims=True)
        gathered = jnp.where(lanes(CZ, BLK) == x, col, gathered)
    sums = jnp.transpose(gathered)[0:EXT] * scale_ref[...]
    out_ref[...] = jnp.zeros(out_ref.shape, f32)
    here = me_ref[1]
    ahead, behind = lax.rem(here + 1, SLICES), lax.rem(here + SLICES - 1, SLICES)
    for m in range(NTM):
        out_ref[here * NTM + m] = sums[HALO + 2 * m : HALO + 2 * m + 2]
        if m < 2:
            out_ref[ahead * NTM + m] = sums[HALO + CX + 2 * m : HALO + CX + 2 * m + 2]
        elif m >= 6:
            out_ref[behind * NTM + m] = sums[2 * m - 12 : 2 * m - 10]


def transform_tables():
    d = np.arange(NT)
    coarse = 2.0 * np.pi * ((np.arange(16)[:, None] * 32 * d) % NT) / NT
    fine = 2.0 * np.pi * ((np.arange(32)[:, None] * d) % NT) / NT
    return [
        jnp.asarray(v.astype(np.float32))
        for v in (np.cos(coarse), np.sin(coarse), np.cos(fine), np.sin(fine))
    ]


def onward(count, k):
    return [(i, (i + k) % count) for i in range(count)]


def body(
    synthetic_traces,
    observed_traces,
    measure_window_start,
    measure_window_end,
    tapers,
    frequency_weight,
    station_receiver_slice,
    station_receiver_cell,
    stiffness,
    attenuation,
    sample_damping_factor,
    forward_wave_field,
):
    me = lax.axis_index("tm").astype(jnp.int32).reshape(1)
    place = jnp.stack([lax.axis_index("tm"), lax.axis_index("cuts")]).astype(jnp.int32)
    syn = jnp.transpose(synthetic_traces, (1, 0, 2))
    obs = jnp.transpose(observed_traces, (1, 0, 2))
    field = jnp.transpose(forward_wave_field, (0, 2, 1, 3))
    win = jnp.concatenate(
        [measure_window_start.T, measure_window_end.T, jnp.zeros((2, BLK), jnp.int32)], axis=0
    )
    routes = [
        [(i, ((i // CORES + k) % CHIPS) * CORES + i % CORES) for i in range(NTM)]
        for k in range(CHIPS)
    ]

    def swap(value):
        return lax.ppermute(value, "tm", [(i, i ^ 1) for i in range(NTM)])

    def along(values):
        return [values[0]] + [lax.ppermute(values[k], "tm", routes[k]) for k in range(1, CHIPS)]

    to_right, to_left = onward(SLICES, 1), onward(SLICES, SLICES - 1)
    sent = shape((CORES, 2 * COMPS, BLK, BLK), bf16)
    parts = call(diff_kernel, [sent] * CHIPS, (me, syn, obs), smem=1, limit=VMEM_ALL)
    near = along(parts)
    slot, codes = call(
        slot_kernel,
        [shape((1, NT), jnp.int32), shape((SLICES, 16, CT), bf16)],
        (station_receiver_slice.reshape(1, NT), station_receiver_cell.reshape(1, NT)),
        after=(parts[0],),
    )
    taps = jnp.pad(tapers, ((0, 3), (0, 0)))
    (oper,) = call(
        operator_kernel,
        [shape((NT, NT), bf16)],
        (frequency_weight.reshape(16, 32), *transform_tables(), taps),
        after=(codes,),
    )
    edge = shape((HALO, COMPS, CZ + 16, BLK), bf16)
    last, first = call(
        edge_kernel,
        [edge, edge],
        (stiffness, attenuation, field),
        scratch=[pltpu.SemaphoreType.DMA((2,))],
        hbm=(2,),
        after=(oper, near[1]),
    )
    left = lax.ppermute(last, "cuts", to_right)
    right = lax.ppermute(first, "cuts", to_left)
    damp = sample_damping_factor.reshape(1, BLK)
    near = [near[0]] + [hold(v, oper) for v in near[1:]]
    far = [swap(v) for v in near]

    adj, misfit, *sends = call(
        owner_kernel,
        [shape((COMPS, BLK, NT), bf16), shape((COMPS, BLK), f32)]
        + [shape((CORES, COMPS, BLK, BLK), bf16)] * CHIPS,
        (me, win, oper, *near, *far),
        scratch=[pltpu.VMEM((CT, NT), bf16), pltpu.VMEM((CT, NT), f32)],
        smem=1,
        after=(codes,),
        limit=VMEM_ALL,
    )
    near = along(sends)
    rows, token = call(
        pick_kernel,
        [shape((SLICES, CAP + 16, CT), bf16), shape((8, BLK), f32)],
        (me, slot, codes, *near, *[swap(v) for v in near]),
        scratch=[pltpu.VMEM((NT, CT), bf16)],
        smem=1,
        after=(left, right),
    )
    rows = lax.all_to_all(rows, "cuts", 0, 0, tiled=True)
    (heads,) = call(
        head_kernel,
        [shape((CZ, BLK), f32)],
        (left, field, right, stiffness, attenuation, damp),
        scratch=[pltpu.VMEM((XGROUP * COMPS * CZ, 2 * BLK), bf16)],
        after=(token,),
    )
    heads = jnp.stack(along([heads] * CHIPS))
    entered, scale = call(
        scan_kernel,
        [shape((COMPS + 1, EXT * CZ, BLK), f32), shape((EXT, CZ), f32)],
        (me, left, field, right, stiffness, attenuation, damp, heads, swap(heads)),
        scratch=[
            pltpu.VMEM((XGROUP * COMPS * CZ, 2 * BLK), bf16),
            pltpu.VMEM((NTM, CZ, BLK), f32),
        ],
        smem=1,
    )
    (terms,) = call(
        sweep_kernel,
        [shape((SLICES * NTM, 2, CZ), f32)],
        (place, rows, entered, scale),
        scratch=[
            pltpu.VMEM((SLICES * CAP, CT), bf16),
            pltpu.VMEM((EXT * CZ, CT), f32),
            pltpu.VMEM((EXT * CZ, BLK), f32),
            pltpu.VMEM((COMPS + 1, EXT * CZ, BLK), f32),
            pltpu.SemaphoreType.DMA,
        ],
        smem=1,
        hbm=(2,),
    )

    terms = lax.all_to_all(terms, ("cuts", "tm"), 0, 0, tiled=True)
    kernel = jnp.sum(terms, axis=0)
    return (jnp.transpose(adj, (1, 0, 2)), misfit.T, kernel)


def solution(mesh):
    return jax.shard_map(
        body,
        mesh=mesh,
        in_specs=(
            P("cuts", None, "tm"),
            P("cuts", None, "tm"),
            P(("cuts", "tm"), None),
            P(("cuts", "tm"), None),
            P(),
            P(),
            P("cuts", None),
            P("cuts"),
            P("cuts", None),
            P("cuts", None),
            P("tm"),
            P("cuts", None, None, "tm"),
        ),
        out_specs=(P(("cuts", "tm"), None, None), P(("cuts", "tm"), None), P(("cuts", "tm"), None)),
        check_vma=False,
    )
```

```python
import math

import jax
import jax.numpy as jnp
import numpy as np
from jax import lax
from jax.experimental import pallas as pl
from jax.experimental.pallas import tpu as pltpu
from jax.sharding import PartitionSpec as P

NT = 1024
SWEEPS = 4
EPSILON = 1e-05
NTM = 8
BLK = 128
COMPS = 3
SLICES = 16
CAP = 128
HALO = 4
CHIPS = 4
CORES = 2
XGROUP = 4
UNROLL = 31
PIECES = [(k, r) for k in range(CHIPS) for r in range(CORES)]
CX = 16
CZ = 128
EXT = CX + 2 * HALO
CT = COMPS * BLK
VMEM_BIG = 52 * 1024 * 1024
VMEM_ALL = 63 * 1024 * 1024

f32 = jnp.float32
bf16 = jnp.bfloat16


def call(kernel, outs, args, scratch=(), smem=0, hbm=(), after=(), limit=VMEM_BIG):
    count = len(args)
    vmem = pl.BlockSpec(memory_space=pltpu.VMEM)
    far = pl.BlockSpec(memory_space=pl.ANY)
    near = pl.BlockSpec(memory_space=pltpu.SMEM)
    specs = [near if i < smem else far if i in hbm else vmem for i in range(count)]

    def inner(*refs):
        kernel(*refs[:count], *refs[count + len(after) :])

    return pl.pallas_call(
        inner,
        out_shape=outs,
        in_specs=specs + [far] * len(after),
        out_specs=[vmem] * len(outs),
        scratch_shapes=list(scratch),
        compiler_params=pltpu.CompilerParams(vmem_limit_bytes=limit),
        cost_estimate=pl.CostEstimate(flops=10**7, bytes_accessed=10**5, transcendentals=0),
    )(*args, *after)


def hold(value, after):
    far = pl.BlockSpec(memory_space=pl.ANY)
    return pl.pallas_call(
        lambda *refs: None,
        out_shape=shape(value.shape, value.dtype),
        in_specs=[far, far],
        out_specs=far,
        input_output_aliases={0: 0},
    )(value, after)


def shape(dims, dtype):
    return jax.ShapeDtypeStruct(dims, dtype)


def block_at(index):
    return pl.ds(pl.multiple_of(index * BLK, BLK), BLK)


def lanes(rows, cols):
    return lax.broadcasted_iota(jnp.int32, (rows, cols), 1)


def columns_of(rows):
    pad = jnp.zeros((BLK - rows.shape[0], BLK), rows.dtype)
    return jnp.transpose(jnp.concatenate([rows, pad], axis=0))


def device_at(me, k, r):
    y, core = me // CORES, me % CORES
    return lax.rem(y + k, CHIPS) * CORES + lax.rem(core + r, CORES)


def diff_kernel(me_ref, syn_ref, obs_ref, *outs):
    me = me_ref[0]
    for k in range(CHIPS):
        for r in range(CORES):
            rows = block_at(device_at(me, k, r))
            for c in range(COMPS):
                syn = syn_ref[c, rows, :]
                outs[k][r, c] = (syn.astype(f32) - obs_ref[c, rows, :].astype(f32)).astype(bf16)
                outs[k][r, COMPS + c] = syn


def edge_kernel(stiff_ref, att_ref, field_ref, last_ref, first_ref, sems):
    copies = []
    for i, (at, edge_ref) in enumerate(((CX - HALO, last_ref), (0, first_ref))):
        copies.append(
            pltpu.make_async_copy(
                field_ref.at[at : at + HALO], edge_ref.at[:, :, 0:CZ], sems.at[i]
            )
        )
        copies[-1].start()
        rows = []
        for ref in (stiff_ref, att_ref):
            rest = ref[at : at + HALO]
            for _ in range(3):
                part = rest.astype(bf16).astype(f32)
                rows.append(part)
                rest = rest - part
        for x in range(HALO):
            tile = [row[x : x + 1] for row in rows]
            tile.append(jnp.zeros((16 - len(rows), CZ), f32))
            tile = jnp.concatenate(tile, axis=0).astype(bf16)
            for c in range(COMPS):
                edge_ref[x, c, CZ : CZ + 16] = tile
    for copy in copies:
        copy.wait()


def operator_kernel(weight_ref, ca_ref, sa_ref, cb_ref, sb_ref, tapers_ref, out_ref):
    hi = lax.Precision.HIGHEST
    w = weight_ref[...]
    wc = jnp.dot(w, cb_ref[...], precision=hi, preferred_element_type=f32)
    ws = jnp.dot(w, sb_ref[...], precision=hi, preferred_element_type=f32)
    h = jnp.sum(ca_ref[...] * wc - sa_ref[...] * ws, axis=0, keepdims=True)
    taps = tapers_ref[...]
    for i in range(NT // BLK):
        wide = jnp.broadcast_to(h, (BLK, NT))
        ring = pltpu.roll(wide, i * BLK, 1, stride=1, stride_axis=0)
        cols = columns_of(taps[:, i * BLK : (i + 1) * BLK])
        joint = cols[:, 0:1] * taps[0:1]
        for k in range(1, 5):
            joint = joint + cols[:, k : k + 1] * taps[k : k + 1]
        out_ref[i * BLK : (i + 1) * BLK, :] = (ring * joint).astype(bf16)


def owner_kernel(me_ref, win_ref, oper_ref, *refs):
    near, far = refs[:CHIPS], refs[CHIPS : 2 * CHIPS]
    adj_ref, mis_ref = refs[2 * CHIPS : 2 * CHIPS + 2]
    sends, (wd_ref, res_ref) = refs[2 * CHIPS + 2 : 3 * CHIPS + 2], refs[3 * CHIPS + 2 :]
    me = me_ref[0]
    win = win_ref[...]
    cols = columns_of(win)
    count = (win[3:6] - win[0:3]).astype(f32)
    lane = lanes(BLK, BLK)
    gathered = jnp.zeros((BLK, BLK), f32)
    for c in range(COMPS):
        squares = jnp.zeros((BLK, BLK), f32)
        for k, r in PIECES:
            tau = device_at(me, CHIPS - k, r)
            block = (far if r else near)[k]
            t = lane + tau * BLK
            inside = (t >= cols[:, c : c + 1]) & (t < cols[:, 3 + c : 4 + c])
            wd_ref[c * BLK : (c + 1) * BLK, block_at(tau)] = jnp.where(
                inside, block[r, c].astype(f32), 0.0
            ).astype(bf16)
            syn = jnp.where(inside, block[r, COMPS + c].astype(f32), 0.0)
            squares = squares + syn * syn
        total = jnp.sum(squares, axis=1, keepdims=True)
        gathered = jnp.where(lane == c, total, gathered)
    energy = jnp.transpose(gathered)[0:3] / count + EPSILON
    scale = columns_of((2.0 / NT) / energy)
    power = jnp.zeros((BLK, BLK), f32)
    t = lanes(BLK, NT)
    res_ref[...] = jnp.dot(wd_ref[...], oper_ref[...], preferred_element_type=f32)
    for c in range(COMPS):
        wd = wd_ref[c * BLK : (c + 1) * BLK]
        res = res_ref[c * BLK : (c + 1) * BLK]
        num = jnp.sum(wd.astype(f32) * res, axis=1, keepdims=True)
        power = jnp.where(lane == c, num, power)
        inside = (t >= cols[:, c : c + 1]) & (t < cols[:, 3 + c : 4 + c])
        adj_ref[c] = jnp.where(inside, res * scale[:, c : c + 1], 0.0).astype(bf16)
    for k, r in PIECES:
        tau = block_at(device_at(me, k, r))
        for c in range(COMPS):
            sends[k][r, c] = adj_ref[c, :, tau]
    mis_ref[...] = jnp.transpose(power)[0:3] / (NT * count * energy)


def slot_kernel(slice_ref, cell_ref, slot_ref, codes_ref):
    n = NT
    slices = slice_ref[...]
    hot = lax.broadcasted_iota(jnp.int32, (SLICES, n), 0) == slices
    before = lax.broadcasted_iota(jnp.int32, (n, n), 0) < lax.broadcasted_iota(jnp.int32, (n, n), 1)
    hot = hot.astype(f32)
    rank = jnp.dot(hot.astype(bf16), before.astype(f32).astype(bf16), preferred_element_type=f32)
    slot = slices * CAP + jnp.sum(hot * rank, axis=0, keepdims=True).astype(jnp.int32)
    slot_ref[...] = slot
    row = lax.broadcasted_iota(jnp.int32, (CAP, n), 0)
    cell = cell_ref[...]
    both = jnp.concatenate(
        [(cell // CZ).astype(f32), (cell % CZ).astype(f32), jnp.zeros((14, n), f32)], axis=0
    ).astype(bf16)
    for s in range(SLICES):
        pick = (row + s * CAP == slot).astype(f32).astype(bf16)
        got = lax.dot_general(both, pick, (((1,), (1,)), ((), ())), preferred_element_type=f32)
        wide = jnp.concatenate([got, jnp.zeros((16, CT - CAP), f32)], axis=1)
        codes_ref[s] = wide.astype(bf16)


def pick_kernel(me_ref, slot_ref, codes_ref, *refs):
    near, far = refs[:CHIPS], refs[CHIPS : 2 * CHIPS]
    out_ref, token_ref, x_ref = refs[2 * CHIPS :]
    token_ref[...] = jnp.zeros((8, BLK), f32)
    me = me_ref[0]
    for k, r in PIECES:
        rows = block_at(device_at(me, CHIPS - k, r))
        for c in range(COMPS):
            x_ref[rows, c * BLK : (c + 1) * BLK] = (far if r else near)[k][r, c]
    slot = slot_ref[...]
    group = 4
    row = lax.broadcasted_iota(jnp.int32, (group * CAP, NT), 0)
    for s in range(0, SLICES, group):
        pick = (row + s * CAP == slot).astype(f32).astype(bf16)
        got = jnp.dot(pick, x_ref[...], preferred_element_type=f32).astype(bf16)
        for i in range(group):
            out_ref[s + i, 0:CAP, :] = got[i * CAP : (i + 1) * CAP]
            out_ref[s + i, CAP : CAP + 16, :] = codes_ref[s + i]


def factors(damp):
    at, to = lax.broadcasted_iota(jnp.int32, (BLK, BLK), 0), lanes(BLK, BLK)
    prod = jnp.where(to > at, pltpu.roll(jnp.broadcast_to(damp, (BLK, BLK)), 1, 1), 1.0)
    for s in (1, 2, 4, 8, 16, 32, 64):
        prod = prod * jnp.where(to < s, 1.0, pltpu.roll(prod, s, 1))
    return jnp.where(to >= at, prod, 0.0)


def halves(value):
    high = value.astype(bf16)
    return high, (value - high.astype(f32)).astype(bf16)


def coefficients(left_ref, right_ref, stiff_ref, att_ref):
    sides = []
    for ref in (left_ref, right_ref):
        tiles = [ref[x, 0, CZ : CZ + 16].astype(f32) for x in range(HALO)]
        sides.append(
            [
                jnp.concatenate(
                    [(t[3 * i : 3 * i + 1] + t[3 * i + 1 : 3 * i + 2]) + t[3 * i + 2 : 3 * i + 3] for t in tiles],
                    axis=0,
                )
                for i in range(2)
            ]
        )
    return [
        jnp.concatenate([sides[0][i], ref[...], sides[1][i]], axis=0)
        for i, ref in enumerate((stiff_ref, att_ref))
    ]


def field_at(left_ref, mid_ref, right_ref, x, c):
    if x < HALO:
        return left_ref[x, c, 0:CZ].astype(f32)
    if x < HALO + CX:
        return mid_ref[x - HALO, c].astype(f32)
    return right_ref[x - HALO - CX, c, 0:CZ].astype(f32)


def head_kernel(
    left_ref, mid_ref, right_ref, stiff_ref, att_ref, damp_ref, head_ref, lhs_ref
):
    lane = lanes(BLK, BLK)
    t = lane.astype(f32)
    damp = damp_ref[...]
    steps = factors(damp)
    att = coefficients(left_ref, right_ref, stiff_ref, att_ref)[1]
    cols = columns_of(jnp.concatenate([att] * COMPS, axis=0))
    column = steps[:, BLK - 1 :] * damp[:, BLK - 1 :]
    high, low = halves(jnp.broadcast_to(column, (BLK, BLK)))
    zero = jnp.zeros((BLK, BLK), bf16)
    mat = jnp.concatenate(
        [jnp.concatenate([high, low], axis=1), jnp.concatenate([high, zero], axis=1)], axis=0
    )
    total = steps[0:1, BLK - 1 :] * damp[:, BLK - 1 :]
    heads = jnp.zeros((BLK, BLK), f32)
    for x0 in range(0, EXT, XGROUP):
        for i in range(XGROUP):
            x = x0 + i
            grow = jnp.exp(cols[:, x : x + 1] * t)
            for c in range(COMPS):
                rows = slice((i * COMPS + c) * CZ, (i * COMPS + c + 1) * CZ)
                high, low = halves(field_at(left_ref, mid_ref, right_ref, x, c) * grow)
                lhs_ref[rows, :BLK] = high
                lhs_ref[rows, BLK:] = low
        got = jnp.dot(lhs_ref[...], mat, preferred_element_type=f32)
        for i in range(XGROUP):
            for c in range(COMPS):
                part = got[(i * COMPS + c) * CZ : (i * COMPS + c + 1) * CZ]
                heads = jnp.where(
                    lane == c * EXT + x0 + i, part[:, :BLK] + part[:, BLK:], heads
                )
    heads = heads * jnp.exp(-float(BLK) * cols)
    head_ref[...] = jnp.where(lane == COMPS * EXT, total, heads)


def column_rows(x):
    return pl.ds((x % 3) * CZ * 8 + x // 3, CZ, stride=8)


def scan_kernel(
    me_ref, left_ref, mid_ref, right_ref, stiff_ref, att_ref, damp_ref, near_ref, far_ref,
    out_ref, scale_ref, lhs_ref, all_ref,
):
    me = me_ref[0]
    lane = lanes(BLK, BLK)
    t = lane.astype(f32)
    y, core = me // CORES, me % CORES
    for k in range(CHIPS):
        chip = lax.rem(y + CHIPS - k, CHIPS) * CORES
        all_ref[chip + core] = near_ref[k]
        all_ref[chip + 1 - core] = far_ref[k]
    stiff, att = coefficients(left_ref, right_ref, stiff_ref, att_ref)
    scale_ref[...] = jnp.sqrt(1.0 - jnp.exp(-2.0 * att)) * (1.0 / math.sqrt(COMPS * NT))
    cols = columns_of(jnp.concatenate([att] * COMPS + [stiff], axis=0))
    whole = jnp.exp(-float(BLK) * cols)
    state = jnp.zeros((BLK, BLK), f32)
    for tau in range(NTM - 1):
        head = all_ref[tau]
        total = head[:, COMPS * EXT : COMPS * EXT + 1]
        state = jnp.where(tau < me, head + whole * total * state, state)
    high, low = halves(factors(damp_ref[...]))
    zero = jnp.zeros((BLK, BLK), bf16)
    mat = jnp.concatenate(
        [jnp.concatenate([high, low], axis=1), jnp.concatenate([high, zero], axis=1)], axis=0
    )
    for x0 in range(0, EXT, XGROUP):
        for i in range(XGROUP):
            x = x0 + i
            grow = jnp.exp(cols[:, x : x + 1] * t)
            for c in range(COMPS):
                rows = slice((i * COMPS + c) * CZ, (i * COMPS + c + 1) * CZ)
                value = field_at(left_ref, mid_ref, right_ref, x, c) * grow
                enter = state[:, c * EXT + x : c * EXT + x + 1]
                high, low = halves(jnp.where(lane == 0, value + enter, value))
                lhs_ref[rows, :BLK] = high
                lhs_ref[rows, BLK:] = low
        got = jnp.dot(lhs_ref[...], mat, preferred_element_type=f32)
        for i in range(XGROUP):
            x = x0 + i
            shrink = jnp.exp(-cols[:, x : x + 1] * t)
            for c in range(COMPS):
                part = got[(i * COMPS + c) * CZ : (i * COMPS + c + 1) * CZ]
                out_ref[c, column_rows(x), :] = (part[:, :BLK] + part[:, BLK:]) * shrink
            at = COMPS * EXT + x
            out_ref[COMPS, column_rows(x), :] = jnp.broadcast_to(cols[:, at : at + 1], (CZ, BLK))


def sweep_kernel(me_ref, got_ref, field_far, scale_ref, *refs):
    out_ref, rows_ref, src_ref, prod_ref, field_ref, sem = refs
    copy = pltpu.make_async_copy(field_far, field_ref, sem)
    copy.start()
    codes = []
    for s in range(SLICES):
        rows_ref[s * CAP : (s + 1) * CAP, :] = got_ref[s, 0:CAP, :]
        codes.append(got_ref[s, CAP : CAP + 16, 0:CAP].astype(f32))
    codes = jnp.concatenate(codes, axis=1)
    wanted = (codes[1:2, :] * 32.0 + codes[0:1, :]).astype(jnp.int32) + HALO
    chunk = 512
    for r0 in range(0, EXT * CZ, chunk):
        at = lax.broadcasted_iota(jnp.int32, (chunk, 1), 0) + r0 % (8 * CZ)
        code = (at // 8) * 32 + 3 * (at % 8) + r0 // (8 * CZ)
        hot = (code == wanted).astype(f32).astype(bf16)
        src_ref[r0 : r0 + chunk, :] = jnp.dot(hot, rows_ref[...], preferred_element_type=f32)
    copy.wait()

    def rows_at(j, z):
        start = (j * CZ + z) * 8
        if not isinstance(start, int):
            start = pl.multiple_of(start, 8)
        return pl.ds(start, 8)

    def update(below, mid, above, z):
        new = []
        for j in range(3):
            after = mid[j + 1] if j < 2 else pltpu.roll(mid[0], 7, 0)
            ahead = mid[j - 1] if j > 0 else pltpu.roll(mid[2], 1, 0)
            around = (after + ahead) + (below[j] + above[j])
            new.append(mid[j] + field_ref[COMPS, rows_at(j, z), :] * (around - 4.0 * mid[j]))
        return tuple(new)

    zero = tuple(jnp.zeros((8, BLK), f32) for _ in range(3))
    for c in range(COMPS):
        cols = slice(c * BLK, (c + 1) * BLK)

        def step(u, held, first=False, past=False, c=c, cols=cols):
            if past and u >= CZ:
                row = zero
            else:
                row = tuple(src_ref[rows_at(j, u), cols] for j in range(3))
            now = []
            for level in range(SWEEPS):
                older, newer = held[level]
                now.append((newer, row))
                z = u - level - 1
                if (first and z < 0) or (past and z >= CZ):
                    row = zero
                    if first:
                        now += list(held[level + 1 :])
                        return tuple(now)
                    continue
                row = update(older, newer, row, z)
            z = u - SWEEPS
            for j in range(3):
                term = row[j] * field_ref[c, rows_at(j, z), :]
                if c > 0:
                    term = term + prod_ref[rows_at(j, z), :]
                prod_ref[rows_at(j, z), :] = term
            return tuple(now)

        held = tuple((zero, zero) for _ in range(SWEEPS))
        for u in range(SWEEPS):
            held = step(u, held, first=True)

        def steps(i, held, step=step):
            for q in range(UNROLL):
                held = step(SWEEPS + i * UNROLL + q, held)
            return held

        held = lax.fori_loop(0, (CZ - SWEEPS) // UNROLL, steps, held)
        for u in range(CZ, CZ + SWEEPS):
            held = step(u, held, past=True)
    gathered = jnp.zeros((CZ, BLK), f32)
    for x in range(EXT):
        col = jnp.sum(prod_ref[column_rows(x), :], axis=1, keepdims=True)
        gathered = jnp.where(lanes(CZ, BLK) == x, col, gathered)
    sums = jnp.transpose(gathered)[0:EXT] * scale_ref[...]
    out_ref[...] = jnp.zeros(out_ref.shape, f32)
    here = me_ref[1]
    ahead, behind = lax.rem(here + 1, SLICES), lax.rem(here + SLICES - 1, SLICES)
    for m in range(NTM):
        out_ref[here * NTM + m] = sums[HALO + 2 * m : HALO + 2 * m + 2]
        if m < 2:
            out_ref[ahead * NTM + m] = sums[HALO + CX + 2 * m : HALO + CX + 2 * m + 2]
        elif m >= 6:
            out_ref[behind * NTM + m] = sums[2 * m - 12 : 2 * m - 10]


def transform_tables():
    d = np.arange(NT)
    coarse = 2.0 * np.pi * ((np.arange(16)[:, None] * 32 * d) % NT) / NT
    fine = 2.0 * np.pi * ((np.arange(32)[:, None] * d) % NT) / NT
    return [
        jnp.asarray(v.astype(np.float32))
        for v in (np.cos(coarse), np.sin(coarse), np.cos(fine), np.sin(fine))
    ]


def onward(count, k):
    return [(i, (i + k) % count) for i in range(count)]


def body(
    synthetic_traces,
    observed_traces,
    measure_window_start,
    measure_window_end,
    tapers,
    frequency_weight,
    station_receiver_slice,
    station_receiver_cell,
    stiffness,
    attenuation,
    sample_damping_factor,
    forward_wave_field,
):
    me = lax.axis_index("tm").astype(jnp.int32).reshape(1)
    place = jnp.stack([lax.axis_index("tm"), lax.axis_index("cuts")]).astype(jnp.int32)
    syn = jnp.transpose(synthetic_traces, (1, 0, 2))
    obs = jnp.transpose(observed_traces, (1, 0, 2))
    field = jnp.transpose(forward_wave_field, (0, 2, 1, 3))
    win = jnp.concatenate(
        [measure_window_start.T, measure_window_end.T, jnp.zeros((2, BLK), jnp.int32)], axis=0
    )
    routes = [
        [(i, ((i // CORES + k) % CHIPS) * CORES + i % CORES) for i in range(NTM)]
        for k in range(CHIPS)
    ]

    def swap(value):
        return lax.ppermute(value, "tm", [(i, i ^ 1) for i in range(NTM)])

    def along(values):
        return [values[0]] + [lax.ppermute(values[k], "tm", routes[k]) for k in range(1, CHIPS)]

    to_right, to_left = onward(SLICES, 1), onward(SLICES, SLICES - 1)
    sent = shape((CORES, 2 * COMPS, BLK, BLK), bf16)
    parts = call(diff_kernel, [sent] * CHIPS, (me, syn, obs), smem=1, limit=VMEM_ALL)
    near = along(parts)
    slot, codes = call(
        slot_kernel,
        [shape((1, NT), jnp.int32), shape((SLICES, 16, CT), bf16)],
        (station_receiver_slice.reshape(1, NT), station_receiver_cell.reshape(1, NT)),
        after=(parts[0],),
    )
    taps = jnp.pad(tapers, ((0, 3), (0, 0)))
    (oper,) = call(
        operator_kernel,
        [shape((NT, NT), bf16)],
        (frequency_weight.reshape(16, 32), *transform_tables(), taps),
        after=(codes,),
    )
    edge = shape((HALO, COMPS, CZ + 16, BLK), bf16)
    last, first = call(
        edge_kernel,
        [edge, edge],
        (stiffness, attenuation, field),
        scratch=[pltpu.SemaphoreType.DMA((2,))],
        hbm=(2,),
        after=(oper,),
    )
    left = lax.ppermute(last, "cuts", to_right)
    right = lax.ppermute(first, "cuts", to_left)
    damp = sample_damping_factor.reshape(1, BLK)
    near = [near[0]] + [hold(v, last) for v in near[1:]]
    far = [swap(v) for v in near]

    adj, misfit, *sends = call(
        owner_kernel,
        [shape((COMPS, BLK, NT), bf16), shape((COMPS, BLK), f32)]
        + [shape((CORES, COMPS, BLK, BLK), bf16)] * CHIPS,
        (me, win, oper, *near, *far),
        scratch=[pltpu.VMEM((CT, NT), bf16), pltpu.VMEM((CT, NT), f32)],
        smem=1,
        after=(codes,),
        limit=VMEM_ALL,
    )
    near = along(sends)
    rows, token = call(
        pick_kernel,
        [shape((SLICES, CAP + 16, CT), bf16), shape((8, BLK), f32)],
        (me, slot, codes, *near, *[swap(v) for v in near]),
        scratch=[pltpu.VMEM((NT, CT), bf16)],
        smem=1,
        after=(left, right),
    )
    rows = lax.all_to_all(rows, "cuts", 0, 0, tiled=True)
    (heads,) = call(
        head_kernel,
        [shape((CZ, BLK), f32)],
        (left, field, right, stiffness, attenuation, damp),
        scratch=[pltpu.VMEM((XGROUP * COMPS * CZ, 2 * BLK), bf16)],
        after=(token,),
    )
    heads = jnp.stack(along([heads] * CHIPS))
    entered, scale = call(
        scan_kernel,
        [shape((COMPS + 1, EXT * CZ, BLK), f32), shape((EXT, CZ), f32)],
        (me, left, field, right, stiffness, attenuation, damp, heads, swap(heads)),
        scratch=[
            pltpu.VMEM((XGROUP * COMPS * CZ, 2 * BLK), bf16),
            pltpu.VMEM((NTM, CZ, BLK), f32),
        ],
        smem=1,
    )
    (terms,) = call(
        sweep_kernel,
        [shape((SLICES * NTM, 2, CZ), f32)],
        (place, rows, entered, scale),
        scratch=[
            pltpu.VMEM((SLICES * CAP, CT), bf16),
            pltpu.VMEM((EXT * CZ, CT), f32),
            pltpu.VMEM((EXT * CZ, BLK), f32),
            pltpu.VMEM((COMPS + 1, EXT * CZ, BLK), f32),
            pltpu.SemaphoreType.DMA,
        ],
        smem=1,
        hbm=(2,),
    )

    terms = lax.all_to_all(terms, ("cuts", "tm"), 0, 0, tiled=True)
    kernel = jnp.sum(terms, axis=0)
    return (jnp.transpose(adj, (1, 0, 2)), misfit.T, kernel)


def solution(mesh):
    return jax.shard_map(
        body,
        mesh=mesh,
        in_specs=(
            P("cuts", None, "tm"),
            P("cuts", None, "tm"),
            P(("cuts", "tm"), None),
            P(("cuts", "tm"), None),
            P(),
            P(),
            P("cuts", None),
            P("cuts"),
            P("cuts", None),
            P("cuts", None),
            P("tm"),
            P("cuts", None, None, "tm"),
        ),
        out_specs=(P(("cuts", "tm"), None, None), P(("cuts", "tm"), None), P(("cuts", "tm"), None)),
        check_vma=False,
    )
```
